512 devices in a mesh: row: 32 (over x_hi, z), col: 16 (over x_lo, y, core).
Axes of the slice: x: 4 (x_hi: 2, x_lo: 2; x = x_hi * 2 + x_lo), y: 4, z: 16, core: 2. Of those that a mesh axis runs over, the one named last changes fastest.
Arguments:
- gradient: float32 [3584, 7168], P('row', 'col'), may hold values from -6 to 6
- moment: float32 [3584, 7168], P('row', 'col'), may hold values from -2 to 2
- second: float32 [3584, 7168], P('row', 'col'), may hold values from 0.05 to 2
- left_basis: bfloat16 [3584, 3584], P('row', 'col'), may hold values from -0.09375 to 0.09375
- right_basis: bfloat16 [7168, 7168], P('row', 'col'), may hold values from -0.0625 to 0.0625
Outputs:
- new_moment: float32 [3584, 7168], P('row', 'col')
- new_second: float32 [3584, 7168], P('row', 'col')
- update: float32 [3584, 7168], P('row', 'col')
The draws below stay inside these ranges and needn't reach their ends.
All inputs are finite; a program needn't handle non-finite values.
Results may differ from the reference program's by a relative error of at most 0.022.
Values may be sent and summed in bfloat16 or wider, within the bound.
A program may use at most 64 MiB of HBM per device.

```python
import math
import jax
import jax.numpy as jnp
from jax import lax

M = 3584
N = 7168
STEP = 100
BLOCK = 448
N_COL = 16


def shard_levels(rng, shape, split, low, high):
    loudness, own = 1.0, jax.random.fold_in(rng, 6)
    for position, parts in split:
        steps = jnp.exp(jax.random.uniform(jax.random.fold_in(own, position), (parts,), jnp.float32, low / len(split), high / len(split)))
        loudness = loudness * jnp.repeat(steps, shape[position] // parts).reshape([-1 if axis == position else 1 for axis in range(len(shape))])
    return loudness


def gaussian(rng, extent, scale, limit, cuts=(), dtype=jnp.bfloat16):
    level = shard_levels(rng, extent, cuts, -0.22, 0.18) if cuts else 1.0
    values = jax.random.normal(rng, extent, jnp.float32) * scale * level
    return jnp.minimum(jnp.maximum(values, -limit), limit).astype(dtype)


def setup_inputs(seed: int = 0) -> dict:
    key_of = jax.random.split(jax.random.key(seed), 6)
    return {
        "gradient": gaussian(key_of[0], (M, N), 1.0, 6.0, ((0, 32), (1, 16)), jnp.float32),
        "moment": gaussian(key_of[1], (M, N), 0.3, 2.0, ((0, 32), (1, 16)), jnp.float32),
        "second": jnp.clip(jnp.exp(math.log(2.0) - 3.6888794 * jax.random.uniform(key_of[2], (M, N), jnp.float32) ** shard_levels(key_of[2], (M, N), ((0, 32), (1, 16)), -0.2, 0.2)), 0.05, 2.0),
        "left_basis": gaussian(key_of[3], (M, M), M ** -0.5, 0.09375, ((0, 32), (1, 16))),
        "right_basis": gaussian(key_of[4], (N, N), N ** -0.5, 0.0625, ((0, 32), (1, 16))),
    }


beta_first = 0.9
beta_second = 0.99
epsilon_add = 1e-08

def reference(gradient, moment, second, left_basis, right_basis):
    low_gradient = gradient.astype(jnp.bfloat16)
    half_rotated = jnp.dot(low_gradient, right_basis, preferred_element_type=jnp.float32).astype(jnp.bfloat16)
    rotated = lax.dot_general(left_basis, half_rotated, (((0,), (0,)), ((), ())), preferred_element_type=jnp.float32)
    new_moment = beta_first * moment + (1.0 - beta_first) * rotated
    new_second = beta_second * second + (1.0 - beta_second) * rotated * rotated
    first_fix = 1.0 - beta_first ** STEP
    second_fix = 1.0 - beta_second ** STEP
    direction = (new_moment / first_fix / (jnp.sqrt(new_second / second_fix) + epsilon_add)).astype(jnp.bfloat16)
    back_rotated = jnp.dot(left_basis, direction, preferred_element_type=jnp.float32).astype(jnp.bfloat16)

    def add_block(number, running):
        offset = (number * BLOCK).astype(jnp.int32)
        back_part = lax.dynamic_slice_in_dim(back_rotated, offset, BLOCK, 1)
        basis_part = lax.dynamic_slice_in_dim(right_basis, offset, BLOCK, 1)
        term = lax.dot_general(back_part, basis_part, (((1,), (1,)), ((), ())), preferred_element_type=jnp.float32)
        rounded = lax.optimization_barrier(term.astype(jnp.bfloat16))
        return running + rounded.astype(jnp.float32)
    update = lax.fori_loop(0, N_COL, add_block, jnp.zeros((M, N), jnp.float32))
    return (new_moment, new_second, update)
```

```python
import functools

import jax
import jax.numpy as jnp
from jax import lax
from jax.experimental import pallas as pl
from jax.experimental.pallas import tpu as pltpu
from jax.sharding import PartitionSpec as P

STEP = 100


beta_first = 0.9
beta_second = 0.99
epsilon_add = 1e-08

F32 = jnp.float32
BF16 = jnp.bfloat16


def optimizer_kernel(
    Z, Y,
    g_ref, m_ref, v_ref, l_ref, r_ref,
    nm_ref, nv_ref, up_ref,
    g_own, g_all, l_all, r_all, part, from_a, from_b, t_own, t_all,
    x_out, x_in, d_all, b_out, b_in, sib_out, sib_in, u_out, u_in,
    g_sem, ls_sem, lr_sem, lfs_sem, lfr_sem, rs_sem, rr_sem,
    tas_sem, tar_sem, tbs_sem, tbr_sem, ts_sem, tr_sem, tfs_sem, tfr_sem,
    x_sem, d_sem_s, d_sem_r, b_sem, ss_sem, sr_sem, us_sem, ur_sem,
):
    C = 2
    K = Y * C
    A, B = Z // 2, Z - 1 - Z // 2
    mr = g_ref.shape[0]
    row, col = lax.axis_index("row"), lax.axis_index("col")
    xh, z = row // Z, lax.rem(row, Z)
    core = lax.rem(col, C)
    y = lax.rem(col // C, Y)
    xl = col // (C * Y)
    sg = 1 - 2 * core
    mine = xh == xl

    def wrap(value):
        return lax.rem(value + 4 * Z, Z)

    def device(dxh, dz, dxl, dy, dcore):
        return {"row": dxh * Z + dz, "col": (dxl * Y + dy) * C + dcore}

    ahead = device(xh, wrap(z + sg), xl, y, core)
    behind = device(xh, wrap(z - sg), xl, y, core)
    partner = device(1 - xh, z, xl, y, core)
    sibling = device(xh, z, xl, y, 1 - core)

    def copy(src, dst, send, recv, target):
        return pltpu.make_async_remote_copy(
            src_ref=src, dst_ref=dst, send_sem=send, recv_sem=recv,
            device_id=target, device_id_type=pl.DeviceIdType.MESH,
        )

    barrier = pltpu.get_barrier_semaphore()

    def greet(target):
        pl.semaphore_signal(barrier, inc=1, device_id=target, device_id_type=pl.DeviceIdType.MESH)

    greet(ahead)
    greet(behind)
    for other in range(1, 4 * K):
        place = lax.rem(xh * 2 * K + col + other, 4 * K)
        greet({"row": (place // (2 * K)) * Z + z, "col": lax.rem(place, 2 * K)})

    g_own[...] = g_ref[...].astype(BF16)
    rows_me = pl.ds(pl.multiple_of(xh * mr, mr), mr)
    g_all[rows_me, :] = g_own[...]
    r_all[z] = r_ref[...]
    slot_me = y * C + core

    @pl.when(mine)
    def _():
        l_all[slot_me, rows_me, :] = l_ref[...]

    pl.semaphore_wait(barrier, 4 * K + 1)

    def to_chips(t):
        dxl, dy = t // Y, t % Y
        here = jnp.logical_and(mine, jnp.logical_and(dxl == xl, dy == y))
        return device(xl, z, dxl, dy, core), jnp.logical_not(here)

    def from_chips(t):
        sxh, sy = t // Y, t % Y
        here = jnp.logical_and(mine, jnp.logical_and(sxh == xh, sy == y))
        return sxh, sy, jnp.logical_not(here)

    def spread(src, dst, send, recv):
        for t in range(2 * Y):
            target, remote = to_chips(t)

            @pl.when(remote)
            def _():
                copy(src, dst.at[slot_me, rows_me, :], send.at[t], recv.at[xh * Y + y], target).start()

    def spread_wait(src, dst, send, recv):
        for t in range(2 * Y):
            target, remote = to_chips(t)

            @pl.when(remote)
            def _():
                copy(src, dst.at[slot_me, rows_me, :], send.at[t], recv.at[0], target).wait_send()

    def share_copy(dst, t, send, recv, c):
        sxh, sy = t // Y, t % Y
        place = dst.at[sy * C + c, pl.ds(sxh * mr, mr), :]
        return copy(place, place, send.at[t], recv.at[t], sibling)

    def share(src, dst, send, recv, fsend, frecv):
        for t in range(2 * Y):
            sxh, sy, remote = from_chips(t)
            place = dst.at[sy * C + core, pl.ds(sxh * mr, mr), :]

            @pl.when(remote)
            def _():
                copy(place, place, send.at[0], recv.at[t], sibling).wait_recv()

            share_copy(dst, t, fsend, frecv, core).start()

    def share_wait(dst, fsend, frecv):
        for t in range(2 * Y):
            share_copy(dst, t, fsend, frecv, 1 - core).wait_recv()

    def share_sent(dst, fsend, frecv):
        for t in range(2 * Y):
            share_copy(dst, t, fsend, frecv, core).wait_send()

    def r_piece(owner, chunk):
        return r_all.at[owner, pl.ds(chunk * mr, mr), :]

    chunks = r_ref.shape[0] // mr

    def r_copy(side, s, chunk):
        if side == 0:
            piece, target = r_piece(wrap(z - sg * (s - 1)), chunk), ahead
        else:
            piece, target = r_piece(wrap(z + sg * (s - 1)), chunk), behind
        index = ((side * A) + s - 1) * chunks + chunk
        return copy(piece, piece, rs_sem.at[index], rr_sem.at[index], target)

    def r_arrival(side, s, chunk):
        piece = r_piece(wrap(z - sg * s) if side == 0 else wrap(z + sg * s), chunk)
        index = ((side * A) + s - 1) * chunks + chunk
        copy(piece, piece, rs_sem.at[index], rr_sem.at[index], ahead).wait_recv()

    def r_step(n):
        s, chunk = n // chunks + 1, n % chunks
        for side, last in ((0, A), (1, B)):
            if s <= last:
                r_arrival(side, s, chunk)
                if s < last:
                    r_copy(side, s + 1, chunk).start()

    for chunk in range(chunks):
        if A:
            r_copy(0, 1, chunk).start()
        if B:
            r_copy(1, 1, chunk).start()
        if chunk == 0:
            g_copy = copy(g_own, g_all.at[rows_me, :], g_sem.at[0], g_sem.at[1], partner)
            g_copy.start()
            spread(l_ref, l_all, ls_sem, lr_sem)
    share(l_ref, l_all, ls_sem, lr_sem, lfs_sem, lfr_sem)
    r_step(0)
    g_copy.wait_recv()
    share_wait(l_all, lfs_sem, lfr_sem)

    per = Z // K

    def part_body(i, _):
        k = lax.rem(z // per + K // 2 + i, K)
        value = lax.dot_general(
            l_all[k], g_all[...], (((0,), (0,)), ((), ())), preferred_element_type=F32
        ).astype(BF16)
        for j in range(per):
            part[k * per + j] = value[j * mr:(j + 1) * mr, :]
        return 0

    lax.fori_loop(0, K, part_body, 0)

    def t_copy(side, s):
        if side == 0:
            d = wrap(z + sg * (A + 1 - s))
            return d, copy(part.at[d], from_a.at[s - 1], tas_sem.at[s - 1], tar_sem.at[s - 1], ahead)
        d = wrap(z - sg * (B + 1 - s))
        return d, copy(part.at[d], from_b.at[s - 1], tbs_sem.at[s - 1], tbr_sem.at[s - 1], behind)

    steps = A * chunks
    done = 1
    for s in range(1, A + 1):
        for side, last, came in ((0, A, from_a), (1, B, from_b)):
            if s <= last:
                d, send = t_copy(side, s)
                if s > 1:
                    t_copy(side, s - 1)[1].wait_recv()
                    part[d] = (part[d].astype(F32) + came[s - 2].astype(F32)).astype(BF16)
                send.start()
        if done < steps:
            r_step(done)
            done += 1
    total = part[z].astype(F32)
    if B:
        t_copy(1, B)[1].wait_recv()
        total = total + from_b[B - 1].astype(F32)
    t_copy(0, A)[1].wait_recv()
    total = total + from_a[A - 1].astype(F32)
    t_own[...] = total.astype(BF16)

    @pl.when(mine)
    def _():
        t_all[slot_me, rows_me, :] = t_own[...]

    spread(t_own, t_all, ts_sem, tr_sem)
    half = (steps - done) // 2
    while done < steps - half:
        r_step(done)
        done += 1
    share(t_own, t_all, ts_sem, tr_sem, tfs_sem, tfr_sem)
    while done < steps:
        r_step(done)
        done += 1
    share_wait(t_all, tfs_sem, tfr_sem)

    nc = r_ref.shape[1]

    def r_block(k):
        return r_all[pl.ds(k * per, per)].reshape(per * r_ref.shape[0], nc)

    acc = jnp.zeros((2 * mr, nc), F32)
    for k in range(K):
        acc = acc + jnp.dot(t_all[k], r_block(k), preferred_element_type=F32)
    x_out[...] = acc
    rows_other = pl.ds(pl.multiple_of((1 - xh) * mr, mr), mr)
    b_out[0:mr, :] = x_out[rows_other, :].astype(BF16)
    x_copy = copy(b_out.at[0:mr, :], x_in, x_sem.at[0], x_sem.at[1], partner)
    x_copy.start()
    x_copy.wait()
    rotated = x_out[rows_me, :] + x_in[...].astype(F32)
    new_moment = beta_first * m_ref[...] + (1.0 - beta_first) * rotated
    new_second = beta_second * v_ref[...] + (1.0 - beta_second) * rotated * rotated
    nm_ref[...] = new_moment
    nv_ref[...] = new_second
    first_fix = 1.0 - beta_first**STEP
    second_fix = 1.0 - beta_second**STEP
    direction = new_moment / first_fix / (jnp.sqrt(new_second / second_fix) + epsilon_add)

    def d_piece(owner):
        return d_all.at[owner // per, pl.ds(pl.multiple_of(lax.rem(owner, per) * mr, mr), mr), :]

    d_all[z // per, pl.ds(pl.multiple_of(lax.rem(z, per) * mr, mr), mr), :] = direction.astype(BF16)

    def d_copy(side, s):
        owner, target = (wrap(z - sg * (s - 1)), ahead) if side == 0 else (wrap(z + sg * (s - 1)), behind)
        index = side * A + s - 1
        piece = d_piece(owner)
        return copy(piece, piece, d_sem_s.at[index], d_sem_r.at[index], target)

    def d_arrival(side, s):
        piece = d_piece(wrap(z - sg * s) if side == 0 else wrap(z + sg * s))
        index = side * A + s - 1
        copy(piece, piece, d_sem_s.at[index], d_sem_r.at[index], ahead).wait_recv()

    for side, last in ((0, A), (1, B)):
        if last:
            d_copy(side, 1).start()
    for s in range(1, A + 1):
        for side, last in ((0, A), (1, B)):
            if s <= last:
                d_arrival(side, s)
                if s < last:
                    d_copy(side, s + 1).start()

    acc = jnp.zeros((2 * mr, nc), F32)
    for k in range(K):
        acc = acc + jnp.dot(l_all[k], d_all[k], preferred_element_type=F32)
    b_out[...] = acc.astype(BF16)
    b_copy = copy(b_out, b_in, b_sem.at[0], b_sem.at[1], partner)
    b_copy.start()
    b_copy.wait_recv()
    back = (acc + b_in[...].astype(F32)).astype(BF16)
    x_out[...] = back.astype(F32)

    def update_block(k):
        return lax.dot_general(
            x_out[...].astype(BF16), r_block(k), (((1,), (1,)), ((), ())), preferred_element_type=F32
        )

    def sib_copy(j):
        return copy(sib_out.at[j], sib_in.at[j], ss_sem.at[j], sr_sem.at[j], sibling)

    for j in range(Y):
        sib_out[j] = update_block(j * C + 1 - core).astype(BF16)
        sib_copy(j).start()

    def u_copy(t):
        txh, ty = t // Y, t % Y
        here = jnp.logical_and(mine, jnp.logical_and(txh == xh, ty == y))
        made = copy(
            u_out.at[ty, pl.ds(txh * mr, mr), :], u_in.at[xl * Y + y],
            us_sem.at[t], ur_sem.at[xl * Y + y], device(txh, z, xh, ty, core),
        )
        return made, here

    for j in range(Y):
        value = update_block(j * C + core)
        sib_copy(j).wait_recv()
        u_out[j] = (value + sib_in[j].astype(F32)).astype(BF16)
        for txh in range(2):
            made, here = u_copy(txh * Y + j)

            @pl.when(jnp.logical_not(here))
            def _():
                made.start()

    @pl.when(mine)
    def _():
        u_in[xl * Y + y] = u_out[y, rows_me, :]

    total = jnp.zeros((mr, nc), F32)
    for t in range(2 * Y):
        here = jnp.logical_and(mine, jnp.logical_and(t // Y == xl, t % Y == y))

        @pl.when(jnp.logical_not(here))
        def _():
            copy(u_in.at[t], u_in.at[t], us_sem.at[0], ur_sem.at[t], sibling).wait_recv()

        total = total + u_in[t].astype(F32)
    up_ref[...] = total

    g_copy.wait_send()
    b_copy.wait_send()
    spread_wait(l_ref, l_all, ls_sem, lr_sem)
    spread_wait(t_own, t_all, ts_sem, tr_sem)
    share_sent(l_all, lfs_sem, lfr_sem)
    share_sent(t_all, tfs_sem, tfr_sem)
    for side, last in ((0, A), (1, B)):
        for s in range(1, last + 1):
            for chunk in range(chunks):
                r_copy(side, s, chunk).wait_send()
            t_copy(side, s)[1].wait_send()
            d_copy(side, s).wait_send()
    for j in range(Y):
        sib_copy(j).wait_send()
    for t in range(2 * Y):
        made, here = u_copy(t)

        @pl.when(jnp.logical_not(here))
        def _():
            made.wait_send()


def per_device(Z, Y, gradient, moment, second, left_basis, right_basis):
    mr, nc = gradient.shape
    K = 2 * Y
    A, B = Z // 2, Z - 1 - Z // 2
    rr = right_basis.shape[0]
    lc = left_basis.shape[1]
    per = Z // K
    chunks = rr // mr
    V = pltpu.VMEM
    DMA = pltpu.SemaphoreType.DMA
    vmem = pl.BlockSpec(memory_space=pltpu.VMEM)
    out = jax.ShapeDtypeStruct((mr, nc), F32)
    return pl.pallas_call(
        functools.partial(optimizer_kernel, Z, Y),
        out_shape=(out, out, out),
        in_specs=[vmem] * 5,
        out_specs=(vmem, vmem, vmem),
        scratch_shapes=[
            V((mr, nc), BF16),
            V((2 * mr, nc), BF16),
            V((K, 2 * mr, lc), BF16),
            V((Z, rr, nc), BF16),
            V((Z, mr, nc), BF16),
            V((A, mr, nc), BF16),
            V((max(B, 1), mr, nc), BF16),
            V((mr, nc), BF16),
            V((K, 2 * mr, nc), BF16),
            V((2 * mr, nc), F32),
            V((mr, nc), BF16),
            V((K, per * mr, nc), BF16),
            V((2 * mr, nc), BF16),
            V((2 * mr, nc), BF16),
            V((Y, 2 * mr, nc), BF16),
            V((Y, 2 * mr, nc), BF16),
            V((Y, 2 * mr, nc), BF16),
            V((2 * Y, mr, nc), BF16),
            DMA((2,)),
            DMA((2 * Y,)), DMA((2 * Y,)), DMA((2 * Y,)), DMA((2 * Y,)),
            DMA(((A + B) * chunks,)), DMA(((A + B) * chunks,)),
            DMA((A,)), DMA((A,)), DMA((max(B, 1),)), DMA((max(B, 1),)),
            DMA((2 * Y,)), DMA((2 * Y,)), DMA((2 * Y,)), DMA((2 * Y,)),
            DMA((2,)),
            DMA((A + B,)), DMA((A + B,)),
            DMA((2,)),
            DMA((Y,)), DMA((Y,)),
            DMA((2 * Y,)), DMA((2 * Y,)),
        ],
        compiler_params=pltpu.CompilerParams(
            collective_id=0, has_side_effects=True, vmem_limit_bytes=48 * 1024 * 1024
        ),
    )(gradient, moment, second, left_basis, right_basis)


def solution(mesh):
    Z, Y = mesh.shape["row"] // 2, mesh.shape["col"] // 4
    return jax.shard_map(
        functools.partial(per_device, Z, Y),
        mesh=mesh,
        in_specs=(
            P("row", "col"),
            P("row", "col"),
            P("row", "col"),
            P("row", "col"),
            P("row", "col"),
        ),
        out_specs=(P("row", "col"), P("row", "col"), P("row", "col")),
        check_vma=False,
    )
```

```python
import functools

import jax
import jax.numpy as jnp
from jax import lax
from jax.experimental import pallas as pl
from jax.experimental.pallas import tpu as pltpu
from jax.sharding import PartitionSpec as P

STEP = 100
R_START = 1
E_EARLY = 0
R_FIRST = True
R_FILL = (1,)


beta_first = 0.9
beta_second = 0.99
epsilon_add = 1e-08

F32 = jnp.float32
BF16 = jnp.bfloat16


def optimizer_kernel(
    Z, Y,
    g_ref, m_ref, v_ref, l_ref, r_ref,
    nm_ref, nv_ref, up_ref,
    g_own, g_all, l_all, r_all, part, from_a, from_b, t_own, t_all,
    g_in, m_in, v_in, l_in, x_out, f_out, f_in, d_own, d_all, b_out, b_in, sib_out, sib_in, u_out, u_in,
    in_sem, out_sem, g_sem, ls_sem, lr_sem, lfs_sem, lfr_sem, rs_sem, rr_sem,
    tas_sem, tar_sem, tbs_sem, tbr_sem, ts_sem, tr_sem, tfs_sem, tfr_sem,
    x_sem, d_sem_s, d_sem_r, b_sem, ss_sem, sr_sem, us_sem, ur_sem, mv_sem,
):
    C = 2
    K = Y * C
    A, B = Z // 2, Z - 1 - Z // 2
    mr = g_ref.shape[0]
    row, col = lax.axis_index("row"), lax.axis_index("col")
    xh, z = row // Z, lax.rem(row, Z)
    core = lax.rem(col, C)
    y = lax.rem(col // C, Y)
    xl = col // (C * Y)
    sg = 1 - 2 * core
    rows_me = pl.ds(pl.multiple_of(xh * mr, mr), mr)
    mine = xh == xl

    def wrap(value):
        return lax.rem(value + 4 * Z, Z)

    def device(dxh, dz, dxl, dy, dcore):
        return {"row": dxh * Z + dz, "col": (dxl * Y + dy) * C + dcore}

    ahead = device(xh, wrap(z + sg), xl, y, core)
    behind = device(xh, wrap(z - sg), xl, y, core)
    partner = device(1 - xh, z, xl, y, core)
    sibling = device(xh, z, xl, y, 1 - core)

    def copy(src, dst, send, recv, target):
        return pltpu.make_async_remote_copy(
            src_ref=src, dst_ref=dst, send_sem=send, recv_sem=recv,
            device_id=target, device_id_type=pl.DeviceIdType.MESH,
        )

    barrier = pltpu.get_barrier_semaphore()

    def greet(target):
        pl.semaphore_signal(barrier, inc=1, device_id=target, device_id_type=pl.DeviceIdType.MESH)

    loads = [
        pltpu.make_async_copy(src, dst, in_sem.at[i])
        for i, (src, dst) in enumerate(
            ((g_ref, g_in), (l_ref, l_in), (r_ref, r_all.at[z]), (m_ref, m_in.at[rows_me, :]), (v_ref, v_in.at[rows_me, :]))
        )
    ]
    for load in loads:
        load.start()
    greet(ahead)
    greet(behind)
    for other in range(1, 4 * K):
        place = lax.rem(xh * 2 * K + col + other, 4 * K)
        greet({"row": (place // (2 * K)) * Z + z, "col": lax.rem(place, 2 * K)})

    loads[0].wait()
    g_own[...] = g_in[...].astype(BF16)
    g_all[rows_me, :] = g_own[...]
    slot_me = y * C + core

    loads[1].wait()

    @pl.when(mine)
    def _():
        l_all[slot_me, rows_me, :] = l_in[...]

    pl.semaphore_wait(barrier, 4 * K + 1)

    def to_chips(t):
        dxl, dy = t // Y, t % Y
        here = jnp.logical_and(mine, jnp.logical_and(dxl == xl, dy == y))
        return device(xl, z, dxl, dy, core), jnp.logical_not(here)

    def from_chips(t):
        sxh, sy = t // Y, t % Y
        here = jnp.logical_and(mine, jnp.logical_and(sxh == xh, sy == y))
        return sxh, sy, jnp.logical_not(here)

    def spread(src, dst, send, recv):
        for t in range(2 * Y):
            target, remote = to_chips(t)

            @pl.when(remote)
            def _():
                copy(src, dst.at[slot_me, rows_me, :], send.at[t], recv.at[xh * Y + y], target).start()

    def spread_wait(src, dst, send, recv):
        for t in range(2 * Y):
            target, remote = to_chips(t)

            @pl.when(remote)
            def _():
                copy(src, dst.at[slot_me, rows_me, :], send.at[t], recv.at[0], target).wait_send()

    def share_copy(dst, t, send, recv, c):
        sxh, sy = t // Y, t % Y
        place = dst.at[sy * C + c, pl.ds(sxh * mr, mr), :]
        return copy(place, place, send.at[t], recv.at[t], sibling)

    def share(src, dst, send, recv, fsend, frecv):
        for t in range(2 * Y):
            sxh, sy, remote = from_chips(t)
            place = dst.at[sy * C + core, pl.ds(sxh * mr, mr), :]

            @pl.when(remote)
            def _():
                copy(place, place, send.at[0], recv.at[t], sibling).wait_recv()

            share_copy(dst, t, fsend, frecv, core).start()

    def share_wait(dst, fsend, frecv):
        for t in range(2 * Y):
            share_copy(dst, t, fsend, frecv, 1 - core).wait_recv()

    def share_sent(dst, fsend, frecv):
        for t in range(2 * Y):
            share_copy(dst, t, fsend, frecv, core).wait_send()

    def r_piece(owner, chunk):
        return r_all.at[owner, pl.ds(chunk * mr, mr), :]

    chunks = r_ref.shape[0] // mr

    def r_copy(side, s, chunk):
        if side == 0:
            piece, target = r_piece(wrap(z - sg * (s - 1)), chunk), ahead
        else:
            piece, target = r_piece(wrap(z + sg * (s - 1)), chunk), behind
        index = ((side * A) + s - 1) * chunks + chunk
        return copy(piece, piece, rs_sem.at[index], rr_sem.at[index], target)

    def r_arrival(side, s, chunk):
        piece = r_piece(wrap(z - sg * s) if side == 0 else wrap(z + sg * s), chunk)
        index = ((side * A) + s - 1) * chunks + chunk
        copy(piece, piece, rs_sem.at[index], rr_sem.at[index], ahead).wait_recv()

    started, arrived = set(), set()

    def r_step(n):
        s, chunk = n // chunks + 1, n % chunks
        for side, last in ((0, A), (1, B)):
            if s <= last:
                r_arrival(side, s, chunk)
                arrived.add((side, s, chunk))
                if s < last:
                    r_copy(side, s + 1, chunk).start()
                    started.add((side, s + 1, chunk))


    def finish(level):
        g_copy.wait_send()
        spread_wait(l_in, l_all, ls_sem, lr_sem)
        share_sent(l_all, lfs_sem, lfr_sem)
        for key in sorted(started - arrived):
            r_arrival(*key)
        for key in sorted(started):
            r_copy(*key).wait_send()
        for side, last in ((0, A), (1, B)):
            for s in range(1, last + 1):
                if level >= 4:
                    t_copy(side, s)[1].wait_send()
                if level >= 8:
                    for i in range(2):
                        d_copy(side, s, i).wait_send()
        if level >= 5:
            spread_wait(t_own, t_all, ts_sem, tr_sem)
            share_sent(t_all, tfs_sem, tfr_sem)
        if 3 <= level < 6:
            for made in moment_copies:
                made.wait()
        if level < 3:
            loads[3].wait()
            loads[4].wait()
        if level >= 6:
            for i in range(2):
                x_copy(i).wait_send()
        if level >= 9:
            b_copy.wait_send()
        if level >= 7:
            for i in range(2):
                for j in range(Y):
                    sib_copy(j, i).wait_send()
                for t in range(2 * Y):
                    made, here = u_copy(t, i)

                    @pl.when(jnp.logical_not(here))
                    def _():
                        made.wait_send()

    g_copy = copy(g_own, g_all.at[rows_me, :], g_sem.at[0], g_sem.at[1], partner)
    if not R_FIRST:
        g_copy.start()
        spread(l_in, l_all, ls_sem, lr_sem)
    loads[2].wait()
    for chunk in range(chunks):
        for side, last in ((0, A), (1, B)):
            if last:
                r_copy(side, 1, chunk).start()
                started.add((side, 1, chunk))
    if R_FIRST:
        g_copy.start()
        spread(l_in, l_all, ls_sem, lr_sem)
    steps = A * chunks
    done = 0

    def r_steps(count):
        nonlocal done
        for _ in range(count):
            if done < steps:
                r_step(done)
                done += 1

    share(l_in, l_all, ls_sem, lr_sem, lfs_sem, lfr_sem)
    r_steps(R_START)
    g_copy.wait_recv()
    share_wait(l_all, lfs_sem, lfr_sem)

    loads[3].wait()
    loads[4].wait()
    moment_copies = [
        copy(m_in.at[rows_me, :], m_in.at[rows_me, :], mv_sem.at[0], mv_sem.at[1], partner),
        copy(v_in.at[rows_me, :], v_in.at[rows_me, :], mv_sem.at[2], mv_sem.at[3], partner),
    ]
    for made in moment_copies:
        made.start()

    per = Z // K

    def part_body(i, _):
        k = lax.rem(z // per + K // 2 + i, K)
        value = lax.dot_general(
            l_all[k], g_all[...], (((0,), (0,)), ((), ())), preferred_element_type=F32
        ).astype(BF16)
        for j in range(per):
            part[k * per + j] = value[j * mr:(j + 1) * mr, :]
        return 0

    lax.fori_loop(0, K, part_body, 0)

    def t_copy(side, s):
        if side == 0:
            d = wrap(z + sg * (A + 1 - s))
            return d, copy(part.at[d], from_a.at[s - 1], tas_sem.at[s - 1], tar_sem.at[s - 1], ahead)
        d = wrap(z - sg * (B + 1 - s))
        return d, copy(part.at[d], from_b.at[s - 1], tbs_sem.at[s - 1], tbr_sem.at[s - 1], behind)

    for s in range(1, A + 1):
        for side, last, came in ((0, A, from_a), (1, B, from_b)):
            if s <= last:
                d, send = t_copy(side, s)
                if s > 1:
                    t_copy(side, s - 1)[1].wait_recv()
                    part[d] = (part[d].astype(F32) + came[s - 2].astype(F32)).astype(BF16)
                send.start()
        r_steps(R_FILL[(s - 1) % len(R_FILL)])
    total = part[z].astype(F32)
    if B:
        t_copy(1, B)[1].wait_recv()
        total = total + from_b[B - 1].astype(F32)
    t_copy(0, A)[1].wait_recv()
    total = total + from_a[A - 1].astype(F32)
    t_own[...] = total.astype(BF16)

    @pl.when(mine)
    def _():
        t_all[slot_me, rows_me, :] = t_own[...]

    spread(t_own, t_all, ts_sem, tr_sem)
    r_steps((steps - done) // 2)
    share(t_own, t_all, ts_sem, tr_sem, tfs_sem, tfr_sem)
    r_steps(steps)
    share_wait(t_all, tfs_sem, tfr_sem)

    nc = r_ref.shape[1]
    split = (nc // 2 + 127) // 128 * 128
    cuts = (slice(0, split), slice(split, nc))

    def x_copy(i):
        return copy(b_out.at[:, cuts[i]], b_in.at[:, cuts[i]], x_sem.at[2 * i], x_sem.at[2 * i + 1], partner)

    for i, cut in enumerate(cuts):
        acc = jnp.zeros((2 * mr, cut.stop - cut.start), F32)
        for k in range(K):
            right = r_all[pl.ds(k * per, per), :, cut].reshape(per * r_ref.shape[0], cut.stop - cut.start)
            acc = acc + jnp.dot(t_all[k], right, preferred_element_type=F32)
        x_out[:, cut] = acc
        b_out[:, cut] = acc.astype(BF16)
        x_copy(i).start()

    first_fix = 1.0 - beta_first**STEP
    second_fix = 1.0 - beta_second**STEP
    for made in moment_copies:
        made.wait()
    for i, cut in enumerate(cuts):
        x_copy(i).wait_recv()
        rotated = x_out[:, cut] + b_in[:, cut].astype(F32)
        new_moment = beta_first * m_in[:, cut] + (1.0 - beta_first) * rotated
        new_second = beta_second * v_in[:, cut] + (1.0 - beta_second) * rotated * rotated
        direction = new_moment / first_fix / (jnp.sqrt(new_second / second_fix) + epsilon_add)
        d_own[:, cut] = direction.astype(BF16)
        m_in[:, cut] = new_moment
        v_in[:, cut] = new_second
    rr = r_ref.shape[0]

    def update_block(k, cut):
        right = r_all[pl.ds(k * per, per)].reshape(per * rr, nc)[cut]
        return lax.dot_general(d_own[...], right, (((1,), (1,)), ((), ())), preferred_element_type=F32)

    def sib_copy(j, i):
        n = j * 2 + i
        return copy(sib_out.at[j, :, cuts[i]], sib_in.at[j, :, cuts[i]], ss_sem.at[n], sr_sem.at[n], sibling)

    for i, cut in enumerate(cuts):
        for j in range(Y):
            sib_out[j, :, cut] = update_block(j * C + 1 - core, cut).astype(BF16)
            sib_copy(j, i).start()

    def u_copy(t, i):
        txh, ty = t // Y, t % Y
        here = jnp.logical_and(mine, jnp.logical_and(txh == xh, ty == y))
        made = copy(
            u_out.at[ty, pl.ds(txh * mr, mr), cuts[i]], u_in.at[xl * Y + y, :, cuts[i]],
            us_sem.at[t * 2 + i], ur_sem.at[(xl * Y + y) * 2 + i], device(txh, z, xh, ty, core),
        )
        return made, here

    for i, cut in enumerate(cuts):
        for j in range(Y):
            value = update_block(j * C + core, cut)
            sib_copy(j, i).wait_recv()
            u_out[j, :, cut] = (value + sib_in[j, :, cut].astype(F32)).astype(BF16)
            for txh in range(2):
                made, here = u_copy(txh * Y + j, i)

                @pl.when(jnp.logical_not(here))
                def _():
                    made.start()

        @pl.when(mine)
        def _():
            u_in[xl * Y + y, :, cut] = u_out[y, rows_me, cut]

    nm_ref[...] = m_in[rows_me, :]
    nv_ref[...] = v_in[rows_me, :]

    def d_piece(owner, i):
        return d_all.at[owner // per, pl.ds(pl.multiple_of(lax.rem(owner, per) * mr, mr), mr), cuts[i]]

    def d_copy(side, s, i):
        owner, target = (wrap(z - sg * (s - 1)), ahead) if side == 0 else (wrap(z + sg * (s - 1)), behind)
        index = (side * A + s - 1) * 2 + i
        piece = d_piece(owner, i)
        return copy(piece, piece, d_sem_s.at[index], d_sem_r.at[index], target)

    def d_step(s, i):
        for side, last in ((0, A), (1, B)):
            if 1 <= s <= last:
                piece = d_piece(wrap(z - sg * s) if side == 0 else wrap(z + sg * s), i)
                index = (side * A + s - 1) * 2 + i
                copy(piece, piece, d_sem_s.at[index], d_sem_r.at[index], ahead).wait_recv()
            if s < last:
                d_copy(side, s + 1, i).start()

    def own_sum(i):
        cut = cuts[i]
        total = jnp.zeros((mr, cut.stop - cut.start), F32)
        for t in range(2 * Y):
            here = jnp.logical_and(mine, jnp.logical_and(t // Y == xl, t % Y == y))

            @pl.when(jnp.logical_not(here))
            def _():
                copy(
                    u_in.at[t, :, cut], u_in.at[t, :, cut], us_sem.at[0], ur_sem.at[t * 2 + i], sibling
                ).wait_recv()

            total = total + u_in[t, :, cut].astype(F32)
        d_all[z // per, pl.ds(pl.multiple_of(lax.rem(z, per) * mr, mr), mr), cut] = total.astype(BF16)

    own_sum(0)
    d_step(0, 0)
    for s in range(1, E_EARLY + 1):
        d_step(s, 0)
    own_sum(1)
    d_step(0, 1)
    for s in range(1, A + 1):
        if s + E_EARLY <= A:
            d_step(s + E_EARLY, 0)
        d_step(s, 1)
    rows_other = pl.ds(pl.multiple_of((1 - xh) * mr, mr), mr)
    acc = jnp.zeros((2 * mr, nc), F32)
    for k in range(K):
        acc = acc + jnp.dot(l_all[k], d_all[k], preferred_element_type=F32)
    x_out[...] = acc
    f_out[...] = x_out[rows_other, :].astype(BF16)
    b_copy = copy(f_out, f_in, b_sem.at[0], b_sem.at[1], partner)
    b_copy.start()
    b_copy.wait_recv()
    up_ref[...] = x_out[rows_me, :] + f_in[...].astype(F32)
    finish(9)


def per_device(Z, Y, gradient, moment, second, left_basis, right_basis):
    mr, nc = gradient.shape
    K = 2 * Y
    A, B = Z // 2, Z - 1 - Z // 2
    rr = right_basis.shape[0]
    lc = left_basis.shape[1]
    per = Z // K
    chunks = rr // mr
    V = pltpu.VMEM
    DMA = pltpu.SemaphoreType.DMA
    vmem = pl.BlockSpec(memory_space=pltpu.VMEM)
    out = jax.ShapeDtypeStruct((mr, nc), F32)
    return pl.pallas_call(
        functools.partial(optimizer_kernel, Z, Y),
        out_shape=(out, out, out),
        in_specs=[pl.BlockSpec(memory_space=pltpu.HBM)] * 5,
        out_specs=(vmem, vmem, vmem),
        scratch_shapes=[
            V((mr, nc), BF16),
            V((2 * mr, nc), BF16),
            V((K, 2 * mr, lc), BF16),
            V((Z, rr, nc), BF16),
            V((Z, mr, nc), BF16),
            V((A, mr, nc), BF16),
            V((max(B, 1), mr, nc), BF16),
            V((mr, nc), BF16),
            V((K, 2 * mr, nc), BF16),
            V((mr, nc), F32),
            V((2 * mr, nc), F32),
            V((2 * mr, nc), F32),
            V((mr, lc), BF16),
            V((2 * mr, nc), F32),
            V((mr, nc), BF16),
            V((mr, nc), BF16),
            V((2 * mr, nc), BF16),
            V((K, per * mr, nc), BF16),
            V((2 * mr, nc), BF16),
            V((2 * mr, nc), BF16),
            V((Y, 2 * mr, nc), BF16),
            V((Y, 2 * mr, nc), BF16),
            V((Y, 2 * mr, nc), BF16),
            V((2 * Y, mr, nc), BF16),
            DMA((5,)),
            DMA((3,)),
            DMA((2,)),
            DMA((2 * Y,)), DMA((2 * Y,)), DMA((2 * Y,)), DMA((2 * Y,)),
            DMA(((A + B) * chunks,)), DMA(((A + B) * chunks,)),
            DMA((A,)), DMA((A,)), DMA((max(B, 1),)), DMA((max(B, 1),)),
            DMA((2 * Y,)), DMA((2 * Y,)), DMA((2 * Y,)), DMA((2 * Y,)),
            DMA((4,)),
            DMA((2 * A + 2 * B,)), DMA((2 * A + 2 * B,)),
            DMA((2,)),
            DMA((2 * Y,)), DMA((2 * Y,)),
            DMA((4 * Y,)), DMA((4 * Y,)),
            DMA((4,)),
        ],
        compiler_params=pltpu.CompilerParams(
            collective_id=0, has_side_effects=True, vmem_limit_bytes=int(63.5 * 1024 * 1024)
        ),
    )(gradient, moment, second, left_basis, right_basis)


def solution(mesh):
    Z, Y = mesh.shape["row"] // 2, mesh.shape["col"] // 4
    return jax.shard_map(
        functools.partial(per_device, Z, Y),
        mesh=mesh,
        in_specs=(
            P("row", "col"),
            P("row", "col"),
            P("row", "col"),
            P("row", "col"),
            P("row", "col"),
        ),
        out_specs=(P("row", "col"), P("row", "col"), P("row", "col")),
        check_vma=False,
    )
```

```python
import functools

import jax
import jax.numpy as jnp
from jax import lax
from jax.experimental import pallas as pl
from jax.experimental.pallas import tpu as pltpu
from jax.sharding import PartitionSpec as P

STEP = 100
R_START = 1
E_EARLY = 0
R_FIRST = True
R_FILL = (1,)


beta_first = 0.9
beta_second = 0.99
epsilon_add = 1e-08

F32 = jnp.float32
BF16 = jnp.bfloat16


def tail_rows(rows):
    return (rows // 2 + 15) // 16 * 16


def packed_rows(rows, columns):
    return columns // 128 * rows + (tail_rows(rows) if columns % 128 else 0)


def pack(dst, value, columns, first=0):
    rows = value.shape[0]
    for start in range(first, first + value.shape[1], 128):
        top, part = start // 128 * rows, value[:, start - first:min(start + 128, columns) - first]
        if start + 128 <= columns:
            dst[top:top + rows, :] = part
        else:
            h = tail_rows(rows)
            dst[top:top + h, 0:64] = part[0:h]
            dst[top:top + rows - h, 64:128] = part[h:rows]


def unpack(dst, src, rows, columns):
    for start in range(0, columns, 128):
        top = start // 128 * rows
        if start + 128 <= columns:
            dst[:, start:start + 128] = src[top:top + rows, :]
        else:
            h = tail_rows(rows)
            dst[0:h, start:columns] = src[top:top + h, 0:64]
            dst[h:rows, start:columns] = src[top:top + rows - h, 64:128]


def optimizer_kernel(
    Z, Y,
    g_ref, m_ref, v_ref, l_ref, r_ref,
    nm_ref, nv_ref, up_ref,
    g_own, g_all, l_all, r_all, r_pk, part, from_a, from_b, t_own, t_pk, t_all,
    g_in, m_in, v_in, l_in, x_out, f_out, f_in, d_own, d_pk, d_all, b_out, b_in, sib_out, sib_in, u_out, u_in,
    in_sem, out_sem, g_sem, ls_sem, lr_sem, lfs_sem, lfr_sem, rs_sem, rr_sem,
    tas_sem, tar_sem, tbs_sem, tbr_sem, ts_sem, tr_sem, tfs_sem, tfr_sem,
    x_sem, d_sem_s, d_sem_r, b_sem, ss_sem, sr_sem, us_sem, ur_sem, mv_sem,
):
    C = 2
    K = Y * C
    A, B = Z // 2, Z - 1 - Z // 2
    mr = g_ref.shape[0]
    rr, nc = r_ref.shape
    pt = packed_rows(mr, nc)
    row, col = lax.axis_index("row"), lax.axis_index("col")
    xh, z = row // Z, lax.rem(row, Z)
    core = lax.rem(col, C)
    y = lax.rem(col // C, Y)
    xl = col // (C * Y)
    sg = 1 - 2 * core
    rows_me = pl.ds(pl.multiple_of(xh * mr, mr), mr)
    mine = xh == xl

    def wrap(value):
        return lax.rem(value + 4 * Z, Z)

    def device(dxh, dz, dxl, dy, dcore):
        return {"row": dxh * Z + dz, "col": (dxl * Y + dy) * C + dcore}

    ahead = device(xh, wrap(z + sg), xl, y, core)
    behind = device(xh, wrap(z - sg), xl, y, core)
    partner = device(1 - xh, z, xl, y, core)
    sibling = device(xh, z, xl, y, 1 - core)

    def copy(src, dst, send, recv, target):
        return pltpu.make_async_remote_copy(
            src_ref=src, dst_ref=dst, send_sem=send, recv_sem=recv,
            device_id=target, device_id_type=pl.DeviceIdType.MESH,
        )

    barrier = pltpu.get_barrier_semaphore()

    def greet(target):
        pl.semaphore_signal(barrier, inc=1, device_id=target, device_id_type=pl.DeviceIdType.MESH)

    loads = [
        pltpu.make_async_copy(src, dst, in_sem.at[i])
        for i, (src, dst) in enumerate(
            ((g_ref, g_in), (l_ref, l_in), (r_ref, r_all.at[z]), (m_ref, m_in.at[rows_me, :]), (v_ref, v_in.at[rows_me, :]))
        )
    ]
    for load in loads:
        load.start()
    greet(ahead)
    greet(behind)
    for other in range(1, 4 * K):
        place = lax.rem(xh * 2 * K + col + other, 4 * K)
        greet({"row": (place // (2 * K)) * Z + z, "col": lax.rem(place, 2 * K)})

    loads[0].wait()
    g_own[...] = g_in[...].astype(BF16)
    g_all[rows_me, :] = g_own[...]
    slot_me = y * C + core

    loads[1].wait()

    @pl.when(mine)
    def _():
        l_all[slot_me, rows_me, :] = l_in[...]

    pl.semaphore_wait(barrier, 4 * K + 1)

    def to_chips(t):
        dxl, dy = t // Y, t % Y
        here = jnp.logical_and(mine, jnp.logical_and(dxl == xl, dy == y))
        return device(xl, z, dxl, dy, core), jnp.logical_not(here)

    def from_chips(t):
        sxh, sy = t // Y, t % Y
        here = jnp.logical_and(mine, jnp.logical_and(sxh == xh, sy == y))
        return sxh, sy, jnp.logical_not(here)

    def half(dst, side):
        rows = dst.shape[1] // 2
        return pl.ds(pl.multiple_of(side * rows, 16), rows)

    def spread(src, dst, send, recv):
        for t in range(2 * Y):
            target, remote = to_chips(t)

            @pl.when(remote)
            def _():
                copy(src, dst.at[slot_me, half(dst, xh), :], send.at[t], recv.at[xh * Y + y], target).start()

    def spread_wait(src, dst, send, recv):
        for t in range(2 * Y):
            target, remote = to_chips(t)

            @pl.when(remote)
            def _():
                copy(src, dst.at[slot_me, half(dst, xh), :], send.at[t], recv.at[0], target).wait_send()

    def share_copy(dst, t, send, recv, c):
        sxh, sy = t // Y, t % Y
        place = dst.at[sy * C + c, half(dst, sxh), :]
        return copy(place, place, send.at[t], recv.at[t], sibling)

    def share(src, dst, send, recv, fsend, frecv):
        for t in range(2 * Y):
            sxh, sy, remote = from_chips(t)
            place = dst.at[sy * C + core, half(dst, sxh), :]

            @pl.when(remote)
            def _():
                copy(place, place, send.at[0], recv.at[t], sibling).wait_recv()

            share_copy(dst, t, fsend, frecv, core).start()

    def share_wait(dst, fsend, frecv):
        for t in range(2 * Y):
            share_copy(dst, t, fsend, frecv, 1 - core).wait_recv()

    def share_sent(dst, fsend, frecv):
        for t in range(2 * Y):
            share_copy(dst, t, fsend, frecv, core).wait_send()

    r_split = (packed_rows(rr, nc) // 2 + 15) // 16 * 16
    r_cuts = ((0, r_split), (r_split, packed_rows(rr, nc) - r_split))
    chunks = 2

    def r_piece(owner, chunk):
        return r_pk.at[owner, pl.ds(*r_cuts[chunk]), :]

    def r_copy(side, s, chunk):
        if side == 0:
            piece, target = r_piece(wrap(z - sg * (s - 1)), chunk), ahead
        else:
            piece, target = r_piece(wrap(z + sg * (s - 1)), chunk), behind
        index = ((side * A) + s - 1) * chunks + chunk
        return copy(piece, piece, rs_sem.at[index], rr_sem.at[index], target)

    def r_arrival(side, s, chunk):
        piece = r_piece(wrap(z - sg * s) if side == 0 else wrap(z + sg * s), chunk)
        index = ((side * A) + s - 1) * chunks + chunk
        copy(piece, piece, rs_sem.at[index], rr_sem.at[index], ahead).wait_recv()

    started, arrived = set(), set()

    def r_step(n):
        s, chunk = n // chunks + 1, n % chunks
        for side, last in ((0, A), (1, B)):
            if s <= last:
                r_arrival(side, s, chunk)
                arrived.add((side, s, chunk))
                if s < last:
                    r_copy(side, s + 1, chunk).start()
                    started.add((side, s + 1, chunk))
                if chunk == chunks - 1:
                    owner = wrap(z - sg * s) if side == 0 else wrap(z + sg * s)
                    unpack(r_all.at[owner], r_pk.at[owner], rr, nc)


    def finish(level):
        g_copy.wait_send()
        spread_wait(l_in, l_all, ls_sem, lr_sem)
        share_sent(l_all, lfs_sem, lfr_sem)
        for key in sorted(started - arrived):
            r_arrival(*key)
        for key in sorted(started):
            r_copy(*key).wait_send()
        for side, last in ((0, A), (1, B)):
            for s in range(1, last + 1):
                if level >= 4:
                    t_copy(side, s)[1].wait_send()
                if level >= 8:
                    for i in range(2):
                        d_copy(side, s, i).wait_send()
        if level >= 5:
            spread_wait(t_own, t_pk, ts_sem, tr_sem)
            share_sent(t_pk, tfs_sem, tfr_sem)
        if 3 <= level < 6:
            for made in moment_copies:
                made.wait()
        if level < 3:
            loads[3].wait()
            loads[4].wait()
        if level >= 6:
            for i in range(2):
                x_copy(i).wait_send()
        if level >= 9:
            b_copy.wait_send()
        if level >= 7:
            for i in range(2):
                for j in range(Y):
                    sib_copy(j, i).wait_send()
                for t in range(2 * Y):
                    made, here = u_copy(t, i)

                    @pl.when(jnp.logical_not(here))
                    def _():
                        made.wait_send()

    g_copy = copy(g_own, g_all.at[rows_me, :], g_sem.at[0], g_sem.at[1], partner)
    if not R_FIRST:
        g_copy.start()
        spread(l_in, l_all, ls_sem, lr_sem)
    loads[2].wait()
    pack(r_pk.at[z], r_all[z], nc)
    for chunk in range(chunks):
        for side, last in ((0, A), (1, B)):
            if last:
                r_copy(side, 1, chunk).start()
                started.add((side, 1, chunk))
    if R_FIRST:
        g_copy.start()
        spread(l_in, l_all, ls_sem, lr_sem)
    steps = A * chunks
    done = 0

    def r_steps(count):
        nonlocal done
        for _ in range(count):
            if done < steps:
                r_step(done)
                done += 1

    share(l_in, l_all, ls_sem, lr_sem, lfs_sem, lfr_sem)
    r_steps(R_START)
    g_copy.wait_recv()
    share_wait(l_all, lfs_sem, lfr_sem)

    loads[3].wait()
    loads[4].wait()
    moment_copies = [
        copy(m_in.at[rows_me, :], m_in.at[rows_me, :], mv_sem.at[0], mv_sem.at[1], partner),
        copy(v_in.at[rows_me, :], v_in.at[rows_me, :], mv_sem.at[2], mv_sem.at[3], partner),
    ]
    for made in moment_copies:
        made.start()

    per = Z // K

    def part_body(i, _):
        k = lax.rem(z // per + K // 2 + i, K)
        value = lax.dot_general(
            l_all[k], g_all[...], (((0,), (0,)), ((), ())), preferred_element_type=F32
        ).astype(BF16)
        for j in range(per):
            pack(part.at[k * per + j], value[j * mr:(j + 1) * mr, :], nc)
        return 0

    lax.fori_loop(0, K, part_body, 0)

    def t_copy(side, s):
        if side == 0:
            d = wrap(z + sg * (A + 1 - s))
            return d, copy(part.at[d], from_a.at[s - 1], tas_sem.at[s - 1], tar_sem.at[s - 1], ahead)
        d = wrap(z - sg * (B + 1 - s))
        return d, copy(part.at[d], from_b.at[s - 1], tbs_sem.at[s - 1], tbr_sem.at[s - 1], behind)

    for s in range(1, A + 1):
        for side, last, came in ((0, A, from_a), (1, B, from_b)):
            if s <= last:
                d, send = t_copy(side, s)
                if s > 1:
                    t_copy(side, s - 1)[1].wait_recv()
                    part[d] = (part[d].astype(F32) + came[s - 2].astype(F32)).astype(BF16)
                send.start()
        r_steps(R_FILL[(s - 1) % len(R_FILL)])
    total = part[z].astype(F32)
    if B:
        t_copy(1, B)[1].wait_recv()
        total = total + from_b[B - 1].astype(F32)
    t_copy(0, A)[1].wait_recv()
    total = total + from_a[A - 1].astype(F32)
    t_own[...] = total.astype(BF16)

    @pl.when(mine)
    def _():
        t_pk[slot_me, half(t_pk, xh), :] = t_own[...]

    spread(t_own, t_pk, ts_sem, tr_sem)
    r_steps((steps - done) // 2)
    share(t_own, t_pk, ts_sem, tr_sem, tfs_sem, tfr_sem)
    share_wait(t_pk, tfs_sem, tfr_sem)
    for k in range(K):
        for side in range(2):
            unpack(t_all.at[k, side * mr:(side + 1) * mr, :], t_pk.at[k, side * pt:(side + 1) * pt, :], mr, nc)
    r_steps(steps)

    split = (nc // 2 + 127) // 128 * 128
    cuts = (slice(0, split), slice(split, nc))

    def x_copy(i):
        return copy(b_out.at[:, cuts[i]], b_in.at[:, cuts[i]], x_sem.at[2 * i], x_sem.at[2 * i + 1], partner)

    for i, cut in enumerate(cuts):
        acc = jnp.zeros((2 * mr, cut.stop - cut.start), F32)
        for k in range(K):
            right = r_all[pl.ds(k * per, per), :, cut].reshape(per * r_ref.shape[0], cut.stop - cut.start)
            acc = acc + jnp.dot(t_all[k], right, preferred_element_type=F32)
        x_out[:, cut] = acc
        b_out[:, cut] = acc.astype(BF16)
        x_copy(i).start()

    first_fix = 1.0 - beta_first**STEP
    second_fix = 1.0 - beta_second**STEP
    for made in moment_copies:
        made.wait()
    for i, cut in enumerate(cuts):
        x_copy(i).wait_recv()
        rotated = x_out[:, cut] + b_in[:, cut].astype(F32)
        new_moment = beta_first * m_in[:, cut] + (1.0 - beta_first) * rotated
        new_second = beta_second * v_in[:, cut] + (1.0 - beta_second) * rotated * rotated
        direction = new_moment / first_fix / (jnp.sqrt(new_second / second_fix) + epsilon_add)
        d_own[:, cut] = direction.astype(BF16)
        m_in[:, cut] = new_moment
        v_in[:, cut] = new_second

    packs = (slice(0, split // 128 * mr), slice(split // 128 * mr, pt))

    def update_block(k, cut):
        right = r_all[pl.ds(k * per, per)].reshape(per * rr, nc)[cut]
        return lax.dot_general(d_own[...], right, (((1,), (1,)), ((), ())), preferred_element_type=F32)

    def sib_copy(j, i):
        n = j * 2 + i
        return copy(sib_out.at[j, :, cuts[i]], sib_in.at[j, :, cuts[i]], ss_sem.at[n], sr_sem.at[n], sibling)

    for i, cut in enumerate(cuts):
        for j in range(Y):
            sib_out[j, :, cut] = update_block(j * C + 1 - core, cut).astype(BF16)
            sib_copy(j, i).start()

    def u_copy(t, i):
        txh, ty = t // Y, t % Y
        here = jnp.logical_and(mine, jnp.logical_and(txh == xh, ty == y))
        made = copy(
            u_out.at[ty, txh, packs[i], :], u_in.at[xl * Y + y, packs[i], :],
            us_sem.at[t * 2 + i], ur_sem.at[(xl * Y + y) * 2 + i], device(txh, z, xh, ty, core),
        )
        return made, here

    for i, cut in enumerate(cuts):
        for j in range(Y):
            value = update_block(j * C + core, cut)
            sib_copy(j, i).wait_recv()
            value = (value + sib_in[j, :, cut].astype(F32)).astype(BF16)
            for txh in range(2):
                pack(u_out.at[j, txh], value[txh * mr:(txh + 1) * mr], nc, cut.start)
            for txh in range(2):
                made, here = u_copy(txh * Y + j, i)

                @pl.when(jnp.logical_not(here))
                def _():
                    made.start()

        @pl.when(mine)
        def _():
            u_in[xl * Y + y, packs[i], :] = u_out[y, xh, packs[i], :]

    nm_ref[...] = m_in[rows_me, :]
    nv_ref[...] = v_in[rows_me, :]

    def d_piece(owner, i):
        return d_pk.at[owner, packs[i], :]

    def d_copy(side, s, i):
        owner, target = (wrap(z - sg * (s - 1)), ahead) if side == 0 else (wrap(z + sg * (s - 1)), behind)
        index = (side * A + s - 1) * 2 + i
        piece = d_piece(owner, i)
        return copy(piece, piece, d_sem_s.at[index], d_sem_r.at[index], target)

    def d_step(s, i):
        for side, last in ((0, A), (1, B)):
            if 1 <= s <= last:
                piece = d_piece(wrap(z - sg * s) if side == 0 else wrap(z + sg * s), i)
                index = (side * A + s - 1) * 2 + i
                copy(piece, piece, d_sem_s.at[index], d_sem_r.at[index], ahead).wait_recv()
            if s < last:
                d_copy(side, s + 1, i).start()
            if i == 1 and 1 <= s <= last:
                owner = wrap(z - sg * s) if side == 0 else wrap(z + sg * s)
                unpack(d_all.at[owner], d_pk.at[owner], mr, nc)

    def own_sum(i):
        rows = packs[i]
        total = jnp.zeros((rows.stop - rows.start, 128), F32)
        for t in range(2 * Y):
            here = jnp.logical_and(mine, jnp.logical_and(t // Y == xl, t % Y == y))

            @pl.when(jnp.logical_not(here))
            def _():
                copy(
                    u_in.at[t, rows, :], u_in.at[t, rows, :], us_sem.at[0], ur_sem.at[t * 2 + i], sibling
                ).wait_recv()

            total = total + u_in[t, rows, :].astype(F32)
        d_pk[z, rows, :] = total.astype(BF16)
        if i == 1:
            unpack(d_all.at[z], d_pk.at[z], mr, nc)

    own_sum(0)
    d_step(0, 0)
    for s in range(1, E_EARLY + 1):
        d_step(s, 0)
    own_sum(1)
    d_step(0, 1)
    for s in range(1, A + 1):
        if s + E_EARLY <= A:
            d_step(s + E_EARLY, 0)
        d_step(s, 1)
    rows_other = pl.ds(pl.multiple_of((1 - xh) * mr, mr), mr)
    acc = jnp.zeros((2 * mr, nc), F32)
    for k in range(K):
        acc = acc + jnp.dot(l_all[k], d_all[pl.ds(k * per, per)].reshape(per * mr, nc), preferred_element_type=F32)
    x_out[...] = acc
    f_out[...] = x_out[rows_other, :].astype(BF16)
    b_copy = copy(f_out, f_in, b_sem.at[0], b_sem.at[1], partner)
    b_copy.start()
    b_copy.wait_recv()
    up_ref[...] = x_out[rows_me, :] + f_in[...].astype(F32)
    finish(9)


def per_device(Z, Y, gradient, moment, second, left_basis, right_basis):
    mr, nc = gradient.shape
    K = 2 * Y
    A, B = Z // 2, Z - 1 - Z // 2
    rr = right_basis.shape[0]
    lc = left_basis.shape[1]
    per = Z // K
    chunks = 2
    pt = packed_rows(mr, nc)
    V = pltpu.VMEM
    DMA = pltpu.SemaphoreType.DMA
    vmem = pl.BlockSpec(memory_space=pltpu.VMEM)
    out = jax.ShapeDtypeStruct((mr, nc), F32)
    return pl.pallas_call(
        functools.partial(optimizer_kernel, Z, Y),
        out_shape=(out, out, out),
        in_specs=[pl.BlockSpec(memory_space=pltpu.HBM)] * 5,
        out_specs=(vmem, vmem, vmem),
        scratch_shapes=[
            V((mr, nc), BF16),
            V((2 * mr, nc), BF16),
            V((K, 2 * mr, lc), BF16),
            V((Z, rr, nc), BF16),
            V((Z, packed_rows(rr, nc), 128), BF16),
            V((Z, pt, 128), BF16),
            V((A, pt, 128), BF16),
            V((max(B, 1), pt, 128), BF16),
            V((pt, 128), BF16),
            V((K, 2 * pt, 128), BF16),
            V((K, 2 * mr, nc), BF16),
            V((mr, nc), F32),
            V((2 * mr, nc), F32),
            V((2 * mr, nc), F32),
            V((mr, lc), BF16),
            V((2 * mr, nc), F32),
            V((mr, nc), BF16),
            V((mr, nc), BF16),
            V((2 * mr, nc), BF16),
            V((Z, pt, 128), BF16),
            V((Z, mr, nc), BF16),
            V((2 * mr, nc), BF16),
            V((2 * mr, nc), BF16),
            V((Y, 2 * mr, nc), BF16),
            V((Y, 2 * mr, nc), BF16),
            V((Y, 2, pt, 128), BF16),
            V((2 * Y, pt, 128), BF16),
            DMA((5,)),
            DMA((3,)),
            DMA((2,)),
            DMA((2 * Y,)), DMA((2 * Y,)), DMA((2 * Y,)), DMA((2 * Y,)),
            DMA(((A + B) * chunks,)), DMA(((A + B) * chunks,)),
            DMA((A,)), DMA((A,)), DMA((max(B, 1),)), DMA((max(B, 1),)),
            DMA((2 * Y,)), DMA((2 * Y,)), DMA((2 * Y,)), DMA((2 * Y,)),
            DMA((4,)),
            DMA((2 * A + 2 * B,)), DMA((2 * A + 2 * B,)),
            DMA((2,)),
            DMA((2 * Y,)), DMA((2 * Y,)),
            DMA((4 * Y,)), DMA((4 * Y,)),
            DMA((4,)),
        ],
        compiler_params=pltpu.CompilerParams(
            collective_id=0, has_side_effects=True, vmem_limit_bytes=int(63.5 * 1024 * 1024)
        ),
    )(gradient, moment, second, left_basis, right_basis)


def solution(mesh):
    Z, Y = mesh.shape["row"] // 2, mesh.shape["col"] // 4
    return jax.shard_map(
        functools.partial(per_device, Z, Y),
        mesh=mesh,
        in_specs=(
            P("row", "col"),
            P("row", "col"),
            P("row", "col"),
            P("row", "col"),
            P("row", "col"),
        ),
        out_specs=(P("row", "col"), P("row", "col"), P("row", "col")),
        check_vma=False,
    )
```

```python
import functools

import jax
import jax.numpy as jnp
from jax import lax
from jax.experimental import pallas as pl
from jax.experimental.pallas import tpu as pltpu
from jax.sharding import PartitionSpec as P

STEP = 100
R_START = 2
R_AFTER = 1
R_MID = 1
E_EARLY = 0
R_FIRST = True
R_FILL = (1,)


beta_first = 0.9
beta_second = 0.99
epsilon_add = 1e-08

F32 = jnp.float32
BF16 = jnp.bfloat16


def tail_rows(rows):
    return (rows // 2 + 15) // 16 * 16


def packed_rows(rows, columns):
    return columns // 128 * rows + (tail_rows(rows) if columns % 128 else 0)


def pack(dst, value, columns, first=0):
    rows = value.shape[0]
    for start in range(first, first + value.shape[1], 128):
        top, part = start // 128 * rows, value[:, start - first:min(start + 128, columns) - first]
        if start + 128 <= columns:
            dst[top:top + rows, :] = part
        else:
            h = tail_rows(rows)
            dst[top:top + h, 0:64] = part[0:h]
            dst[top:top + rows - h, 64:128] = part[h:rows]


def unpack(dst, src, rows, columns):
    for start in range(0, columns, 128):
        top = start // 128 * rows
        if start + 128 <= columns:
            dst[:, start:start + 128] = src[top:top + rows, :]
        else:
            h = tail_rows(rows)
            dst[0:h, start:columns] = src[top:top + h, 0:64]
            dst[h:rows, start:columns] = src[top:top + rows - h, 64:128]


def optimizer_kernel(
    Z, Y,
    g_ref, m_ref, v_ref, l_ref, r_ref,
    nm_ref, nv_ref, up_ref,
    g_own, g_all, l_all, r_all, r_pk, part, from_a, from_b, t_own, t_pk, t_all,
    g_in, m_in, v_in, l_in, x_out, f_out, f_in, d_own, d_pk, d_all, b_out, b_in, sib_out, sib_in, u_out, u_in,
    in_sem, out_sem, g_sem, ls_sem, lr_sem, lfs_sem, lfr_sem, rs_sem, rr_sem,
    tas_sem, tar_sem, tbs_sem, tbr_sem, ts_sem, tr_sem, tfs_sem, tfr_sem,
    x_sem, d_sem_s, d_sem_r, b_sem, ss_sem, sr_sem, us_sem, ur_sem, mv_sem,
):
    C = 2
    K = Y * C
    A, B = Z // 2, Z - 1 - Z // 2
    mr = g_ref.shape[0]
    rr, nc = r_ref.shape
    pt = packed_rows(mr, nc)
    row, col = lax.axis_index("row"), lax.axis_index("col")
    xh, z = row // Z, lax.rem(row, Z)
    core = lax.rem(col, C)
    y = lax.rem(col // C, Y)
    xl = col // (C * Y)
    sg = 1 - 2 * core
    rows_me = pl.ds(pl.multiple_of(xh * mr, mr), mr)
    mine = xh == xl

    def wrap(value):
        return lax.rem(value + 4 * Z, Z)

    def device(dxh, dz, dxl, dy, dcore):
        return {"row": dxh * Z + dz, "col": (dxl * Y + dy) * C + dcore}

    ahead = device(xh, wrap(z + sg), xl, y, core)
    behind = device(xh, wrap(z - sg), xl, y, core)
    partner = device(1 - xh, z, xl, y, core)
    sibling = device(xh, z, xl, y, 1 - core)

    def copy(src, dst, send, recv, target):
        return pltpu.make_async_remote_copy(
            src_ref=src, dst_ref=dst, send_sem=send, recv_sem=recv,
            device_id=target, device_id_type=pl.DeviceIdType.MESH,
        )

    barrier = pltpu.get_barrier_semaphore()

    def greet(target):
        pl.semaphore_signal(barrier, inc=1, device_id=target, device_id_type=pl.DeviceIdType.MESH)

    loads = [
        pltpu.make_async_copy(src, dst, in_sem.at[i])
        for i, (src, dst) in enumerate(
            ((g_ref, g_in), (l_ref, l_in), (r_ref, r_all.at[z]), (m_ref, m_in.at[rows_me, :]), (v_ref, v_in.at[rows_me, :]))
        )
    ]
    for load in loads:
        load.start()
    greet(ahead)
    greet(behind)
    for other in range(1, 4 * K):
        place = lax.rem(xh * 2 * K + col + other, 4 * K)
        greet({"row": (place // (2 * K)) * Z + z, "col": lax.rem(place, 2 * K)})

    loads[0].wait()
    g_own[...] = g_in[...].astype(BF16)
    g_all[rows_me, :] = g_own[...]
    slot_me = y * C + core

    loads[1].wait()

    @pl.when(mine)
    def _():
        l_all[slot_me, rows_me, :] = l_in[...]

    pl.semaphore_wait(barrier, 4 * K + 1)

    def to_chips(t):
        dxl, dy = t // Y, t % Y
        here = jnp.logical_and(mine, jnp.logical_and(dxl == xl, dy == y))
        return device(xl, z, dxl, dy, core), jnp.logical_not(here)

    def from_chips(t):
        sxh, sy = t // Y, t % Y
        here = jnp.logical_and(mine, jnp.logical_and(sxh == xh, sy == y))
        return sxh, sy, jnp.logical_not(here)

    def half(dst, side):
        rows = dst.shape[1] // 2
        return pl.ds(pl.multiple_of(side * rows, 16), rows)

    def spread(src, dst, send, recv):
        for t in range(2 * Y):
            target, remote = to_chips(t)

            @pl.when(remote)
            def _():
                copy(src, dst.at[slot_me, half(dst, xh), :], send.at[t], recv.at[xh * Y + y], target).start()

    def spread_wait(src, dst, send, recv):
        for t in range(2 * Y):
            target, remote = to_chips(t)

            @pl.when(remote)
            def _():
                copy(src, dst.at[slot_me, half(dst, xh), :], send.at[t], recv.at[0], target).wait_send()

    def share_copy(dst, t, send, recv, c):
        sxh, sy = t // Y, t % Y
        place = dst.at[sy * C + c, half(dst, sxh), :]
        return copy(place, place, send.at[t], recv.at[t], sibling)

    def share(src, dst, send, recv, fsend, frecv):
        for t in range(2 * Y):
            sxh, sy, remote = from_chips(t)
            place = dst.at[sy * C + core, half(dst, sxh), :]

            @pl.when(remote)
            def _():
                copy(place, place, send.at[0], recv.at[t], sibling).wait_recv()

            share_copy(dst, t, fsend, frecv, core).start()

    def share_wait(dst, fsend, frecv):
        for t in range(2 * Y):
            share_copy(dst, t, fsend, frecv, 1 - core).wait_recv()

    def share_sent(dst, fsend, frecv):
        for t in range(2 * Y):
            share_copy(dst, t, fsend, frecv, core).wait_send()

    r_split = (packed_rows(rr, nc) // 2 + 15) // 16 * 16
    r_cuts = ((0, r_split), (r_split, packed_rows(rr, nc) - r_split))
    chunks = 2

    def r_piece(owner, chunk):
        return r_pk.at[owner, pl.ds(*r_cuts[chunk]), :]

    def r_copy(side, s, chunk):
        if side == 0:
            piece, target = r_piece(wrap(z - sg * (s - 1)), chunk), ahead
        else:
            piece, target = r_piece(wrap(z + sg * (s - 1)), chunk), behind
        index = ((side * A) + s - 1) * chunks + chunk
        return copy(piece, piece, rs_sem.at[index], rr_sem.at[index], target)

    def r_arrival(side, s, chunk):
        piece = r_piece(wrap(z - sg * s) if side == 0 else wrap(z + sg * s), chunk)
        index = ((side * A) + s - 1) * chunks + chunk
        copy(piece, piece, rs_sem.at[index], rr_sem.at[index], ahead).wait_recv()

    started, arrived = set(), set()

    def r_step(n):
        s, chunk = n // chunks + 1, n % chunks
        for side, last in ((0, A), (1, B)):
            if s <= last:
                r_arrival(side, s, chunk)
                arrived.add((side, s, chunk))
                if s < last:
                    r_copy(side, s + 1, chunk).start()
                    started.add((side, s + 1, chunk))
                if chunk == chunks - 1:
                    owner = wrap(z - sg * s) if side == 0 else wrap(z + sg * s)
                    unpack(r_all.at[owner], r_pk.at[owner], rr, nc)


    def finish(level):
        g_copy.wait_send()
        spread_wait(l_in, l_all, ls_sem, lr_sem)
        share_sent(l_all, lfs_sem, lfr_sem)
        for key in sorted(started - arrived):
            r_arrival(*key)
        for key in sorted(started):
            r_copy(*key).wait_send()
        for side, last in ((0, A), (1, B)):
            for s in range(1, last + 1):
                if level >= 4:
                    for i in range(2):
                        t_copy(side, s, i)[1].wait_send()
                if level >= 8:
                    for i in range(2):
                        d_copy(side, s, i).wait_send()
        if level >= 5:
            spread_wait(t_own, t_pk, ts_sem, tr_sem)
            share_sent(t_pk, tfs_sem, tfr_sem)
        if 3 <= level < 6:
            for made in moment_copies:
                made.wait()
        if level < 3:
            loads[3].wait()
            loads[4].wait()
        if level >= 6:
            for i in range(2):
                x_copy(i).wait_send()
        if level >= 9:
            b_copy.wait_send()
        if level >= 7:
            for i in range(2):
                for j in range(Y):
                    sib_copy(j, i).wait_send()
                for t in range(2 * Y):
                    made, here = u_copy(t, i)

                    @pl.when(jnp.logical_not(here))
                    def _():
                        made.wait_send()

    g_copy = copy(g_own, g_all.at[rows_me, :], g_sem.at[0], g_sem.at[1], partner)
    if not R_FIRST:
        g_copy.start()
        spread(l_in, l_all, ls_sem, lr_sem)
    loads[2].wait()
    pack(r_pk.at[z], r_all[z], nc)
    for chunk in range(chunks):
        for side, last in ((0, A), (1, B)):
            if last:
                r_copy(side, 1, chunk).start()
                started.add((side, 1, chunk))
    if R_FIRST:
        g_copy.start()
        spread(l_in, l_all, ls_sem, lr_sem)
    steps = A * chunks
    done = 0

    def r_steps(count):
        nonlocal done
        for _ in range(count):
            if done < steps:
                r_step(done)
                done += 1

    share(l_in, l_all, ls_sem, lr_sem, lfs_sem, lfr_sem)
    r_steps(R_START)
    g_copy.wait_recv()
    share_wait(l_all, lfs_sem, lfr_sem)

    loads[3].wait()
    loads[4].wait()
    moment_copies = [
        copy(m_in.at[rows_me, :], m_in.at[rows_me, :], mv_sem.at[0], mv_sem.at[1], partner),
        copy(v_in.at[rows_me, :], v_in.at[rows_me, :], mv_sem.at[2], mv_sem.at[3], partner),
    ]
    for made in moment_copies:
        made.start()

    per = Z // K

    def part_body(i, _):
        k = lax.rem(z // per + K // 2 + i, K)
        value = lax.dot_general(
            l_all[k], g_all[...], (((0,), (0,)), ((), ())), preferred_element_type=F32
        ).astype(BF16)
        for j in range(per):
            pack(part.at[k * per + j], value[j * mr:(j + 1) * mr, :], nc)
        return 0

    lax.fori_loop(0, K, part_body, 0)

    t_half = (pt // 2 + 15) // 16 * 16
    t_cuts = (slice(0, t_half), slice(t_half, pt))

    def t_copy(side, s, i):
        rows, n = t_cuts[i], (s - 1) * 2 + i
        if side == 0:
            d = wrap(z + sg * (A + 1 - s))
            return d, copy(part.at[d, rows, :], from_a.at[s - 1, rows, :], tas_sem.at[n], tar_sem.at[n], ahead)
        d = wrap(z - sg * (B + 1 - s))
        return d, copy(part.at[d, rows, :], from_b.at[s - 1, rows, :], tbs_sem.at[n], tbr_sem.at[n], behind)

    for s in range(1, A + 1):
        for i, rows in enumerate(t_cuts):
            for side, last, came in ((0, A, from_a), (1, B, from_b)):
                if s <= last:
                    d, send = t_copy(side, s, i)
                    if s > 1:
                        t_copy(side, s - 1, i)[1].wait_recv()
                        part[d, rows, :] = (
                            part[d, rows, :].astype(F32) + came[s - 2, rows, :].astype(F32)
                        ).astype(BF16)
                    send.start()
            if i == R_AFTER:
                r_steps(R_FILL[(s - 1) % len(R_FILL)])
    for i, rows in enumerate(t_cuts):
        total = part[z, rows, :].astype(F32)
        if B:
            t_copy(1, B, i)[1].wait_recv()
            total = total + from_b[B - 1, rows, :].astype(F32)
        t_copy(0, A, i)[1].wait_recv()
        total = total + from_a[A - 1, rows, :].astype(F32)
        t_own[rows, :] = total.astype(BF16)

    @pl.when(mine)
    def _():
        t_pk[slot_me, half(t_pk, xh), :] = t_own[...]

    spread(t_own, t_pk, ts_sem, tr_sem)
    r_steps((steps - done) // R_MID if R_MID else 0)
    share(t_own, t_pk, ts_sem, tr_sem, tfs_sem, tfr_sem)
    share_wait(t_pk, tfs_sem, tfr_sem)
    for k in range(K):
        for side in range(2):
            unpack(t_all.at[k, side * mr:(side + 1) * mr, :], t_pk.at[k, side * pt:(side + 1) * pt, :], mr, nc)
    r_steps(steps)

    split = (nc // 2 + 127) // 128 * 128
    cuts = (slice(0, split), slice(split, nc))

    def x_copy(i):
        return copy(b_out.at[:, cuts[i]], b_in.at[:, cuts[i]], x_sem.at[2 * i], x_sem.at[2 * i + 1], partner)

    for i, cut in enumerate(cuts):
        acc = jnp.zeros((2 * mr, cut.stop - cut.start), F32)
        for k in range(K):
            right = r_all[pl.ds(k * per, per), :, cut].reshape(per * r_ref.shape[0], cut.stop - cut.start)
            acc = acc + jnp.dot(t_all[k], right, preferred_element_type=F32)
        x_out[:, cut] = acc
        b_out[:, cut] = acc.astype(BF16)
        x_copy(i).start()

    first_fix = 1.0 - beta_first**STEP
    second_fix = 1.0 - beta_second**STEP
    for made in moment_copies:
        made.wait()
    for i, cut in enumerate(cuts):
        x_copy(i).wait_recv()
        rotated = x_out[:, cut] + b_in[:, cut].astype(F32)
        new_moment = beta_first * m_in[:, cut] + (1.0 - beta_first) * rotated
        new_second = beta_second * v_in[:, cut] + (1.0 - beta_second) * rotated * rotated
        direction = new_moment / first_fix / (jnp.sqrt(new_second / second_fix) + epsilon_add)
        d_own[:, cut] = direction.astype(BF16)
        m_in[:, cut] = new_moment
        v_in[:, cut] = new_second

    packs = (slice(0, split // 128 * mr), slice(split // 128 * mr, pt))

    def update_block(k, cut):
        right = r_all[pl.ds(k * per, per)].reshape(per * rr, nc)[cut]
        return lax.dot_general(d_own[...], right, (((1,), (1,)), ((), ())), preferred_element_type=F32)

    def sib_copy(j, i):
        n = j * 2 + i
        return copy(sib_out.at[j, :, cuts[i]], sib_in.at[j, :, cuts[i]], ss_sem.at[n], sr_sem.at[n], sibling)

    for i, cut in enumerate(cuts):
        for j in range(Y):
            sib_out[j, :, cut] = update_block(j * C + 1 - core, cut).astype(BF16)
            sib_copy(j, i).start()

    def u_copy(t, i):
        txh, ty = t // Y, t % Y
        here = jnp.logical_and(mine, jnp.logical_and(txh == xh, ty == y))
        made = copy(
            u_out.at[ty, txh, packs[i], :], u_in.at[xl * Y + y, packs[i], :],
            us_sem.at[t * 2 + i], ur_sem.at[(xl * Y + y) * 2 + i], device(txh, z, xh, ty, core),
        )
        return made, here

    for i, cut in enumerate(cuts):
        for j in range(Y):
            value = update_block(j * C + core, cut)
            sib_copy(j, i).wait_recv()
            value = (value + sib_in[j, :, cut].astype(F32)).astype(BF16)
            for txh in range(2):
                pack(u_out.at[j, txh], value[txh * mr:(txh + 1) * mr], nc, cut.start)
            for txh in range(2):
                made, here = u_copy(txh * Y + j, i)

                @pl.when(jnp.logical_not(here))
                def _():
                    made.start()

        @pl.when(mine)
        def _():
            u_in[xl * Y + y, packs[i], :] = u_out[y, xh, packs[i], :]

    nm_ref[...] = m_in[rows_me, :]
    nv_ref[...] = v_in[rows_me, :]

    def d_piece(owner, i):
        return d_pk.at[owner, packs[i], :]

    def d_copy(side, s, i):
        owner, target = (wrap(z - sg * (s - 1)), ahead) if side == 0 else (wrap(z + sg * (s - 1)), behind)
        index = (side * A + s - 1) * 2 + i
        piece = d_piece(owner, i)
        return copy(piece, piece, d_sem_s.at[index], d_sem_r.at[index], target)

    def d_step(s, i):
        for side, last in ((0, A), (1, B)):
            if 1 <= s <= last:
                piece = d_piece(wrap(z - sg * s) if side == 0 else wrap(z + sg * s), i)
                index = (side * A + s - 1) * 2 + i
                copy(piece, piece, d_sem_s.at[index], d_sem_r.at[index], ahead).wait_recv()
            if s < last:
                d_copy(side, s + 1, i).start()
            if i == 1 and 1 <= s <= last:
                owner = wrap(z - sg * s) if side == 0 else wrap(z + sg * s)
                unpack(d_all.at[owner], d_pk.at[owner], mr, nc)

    def own_sum(i):
        rows = packs[i]
        total = jnp.zeros((rows.stop - rows.start, 128), F32)
        for t in range(2 * Y):
            here = jnp.logical_and(mine, jnp.logical_and(t // Y == xl, t % Y == y))

            @pl.when(jnp.logical_not(here))
            def _():
                copy(
                    u_in.at[t, rows, :], u_in.at[t, rows, :], us_sem.at[0], ur_sem.at[t * 2 + i], sibling
                ).wait_recv()

            total = total + u_in[t, rows, :].astype(F32)
        d_pk[z, rows, :] = total.astype(BF16)
        if i == 1:
            unpack(d_all.at[z], d_pk.at[z], mr, nc)

    own_sum(0)
    d_step(0, 0)
    for s in range(1, E_EARLY + 1):
        d_step(s, 0)
    own_sum(1)
    d_step(0, 1)
    for s in range(1, A + 1):
        if s + E_EARLY <= A:
            d_step(s + E_EARLY, 0)
        d_step(s, 1)
    rows_other = pl.ds(pl.multiple_of((1 - xh) * mr, mr), mr)
    acc = jnp.zeros((2 * mr, nc), F32)
    for k in range(K):
        acc = acc + jnp.dot(l_all[k], d_all[pl.ds(k * per, per)].reshape(per * mr, nc), preferred_element_type=F32)
    x_out[...] = acc
    f_out[...] = x_out[rows_other, :].astype(BF16)
    b_copy = copy(f_out, f_in, b_sem.at[0], b_sem.at[1], partner)
    b_copy.start()
    b_copy.wait_recv()
    up_ref[...] = x_out[rows_me, :] + f_in[...].astype(F32)
    finish(9)


def per_device(Z, Y, gradient, moment, second, left_basis, right_basis):
    mr, nc = gradient.shape
    K = 2 * Y
    A, B = Z // 2, Z - 1 - Z // 2
    rr = right_basis.shape[0]
    lc = left_basis.shape[1]
    per = Z // K
    chunks = 2
    pt = packed_rows(mr, nc)
    V = pltpu.VMEM
    DMA = pltpu.SemaphoreType.DMA
    vmem = pl.BlockSpec(memory_space=pltpu.VMEM)
    out = jax.ShapeDtypeStruct((mr, nc), F32)
    return pl.pallas_call(
        functools.partial(optimizer_kernel, Z, Y),
        out_shape=(out, out, out),
        in_specs=[pl.BlockSpec(memory_space=pltpu.HBM)] * 5,
        out_specs=(vmem, vmem, vmem),
        scratch_shapes=[
            V((mr, nc), BF16),
            V((2 * mr, nc), BF16),
            V((K, 2 * mr, lc), BF16),
            V((Z, rr, nc), BF16),
            V((Z, packed_rows(rr, nc), 128), BF16),
            V((Z, pt, 128), BF16),
            V((A, pt, 128), BF16),
            V((max(B, 1), pt, 128), BF16),
            V((pt, 128), BF16),
            V((K, 2 * pt, 128), BF16),
            V((K, 2 * mr, nc), BF16),
            V((mr, nc), F32),
            V((2 * mr, nc), F32),
            V((2 * mr, nc), F32),
            V((mr, lc), BF16),
            V((2 * mr, nc), F32),
            V((mr, nc), BF16),
            V((mr, nc), BF16),
            V((2 * mr, nc), BF16),
            V((Z, pt, 128), BF16),
            V((Z, mr, nc), BF16),
            V((2 * mr, nc), BF16),
            V((2 * mr, nc), BF16),
            V((Y, 2 * mr, nc), BF16),
            V((Y, 2 * mr, nc), BF16),
            V((Y, 2, pt, 128), BF16),
            V((2 * Y, pt, 128), BF16),
            DMA((5,)),
            DMA((3,)),
            DMA((2,)),
            DMA((2 * Y,)), DMA((2 * Y,)), DMA((2 * Y,)), DMA((2 * Y,)),
            DMA(((A + B) * chunks,)), DMA(((A + B) * chunks,)),
            DMA((2 * A,)), DMA((2 * A,)), DMA((2 * max(B, 1),)), DMA((2 * max(B, 1),)),
            DMA((2 * Y,)), DMA((2 * Y,)), DMA((2 * Y,)), DMA((2 * Y,)),
            DMA((4,)),
            DMA((2 * A + 2 * B,)), DMA((2 * A + 2 * B,)),
            DMA((2,)),
            DMA((2 * Y,)), DMA((2 * Y,)),
            DMA((4 * Y,)), DMA((4 * Y,)),
            DMA((4,)),
        ],
        compiler_params=pltpu.CompilerParams(
            collective_id=0, has_side_effects=True, vmem_limit_bytes=int(63.5 * 1024 * 1024)
        ),
    )(gradient, moment, second, left_basis, right_basis)


def solution(mesh):
    Z, Y = mesh.shape["row"] // 2, mesh.shape["col"] // 4
    return jax.shard_map(
        functools.partial(per_device, Z, Y),
        mesh=mesh,
        in_specs=(
            P("row", "col"),
            P("row", "col"),
            P("row", "col"),
            P("row", "col"),
            P("row", "col"),
        ),
        out_specs=(P("row", "col"), P("row", "col"), P("row", "col")),
        check_vma=False,
    )
```

```python
import functools

import jax
import jax.numpy as jnp
from jax import lax
from jax.experimental import pallas as pl
from jax.experimental.pallas import tpu as pltpu
from jax.sharding import PartitionSpec as P

STEP = 100
R_START = 2
R_MID = 1
T_N = 1
E_EARLY = 0
R_FIRST = True
R_FILL = (1,)


beta_first = 0.9
beta_second = 0.99
epsilon_add = 1e-08

F32 = jnp.float32
BF16 = jnp.bfloat16


def tail_rows(rows):
    return (rows // 2 + 15) // 16 * 16


def packed_rows(rows, columns):
    return columns // 128 * rows + (tail_rows(rows) if columns % 128 else 0)


def pack(dst, value, columns, first=0):
    rows = value.shape[0]
    for start in range(first, first + value.shape[1], 128):
        top, part = start // 128 * rows, value[:, start - first:min(start + 128, columns) - first]
        if start + 128 <= columns:
            dst[top:top + rows, :] = part
        else:
            h = tail_rows(rows)
            dst[top:top + h, 0:64] = part[0:h]
            dst[top:top + rows - h, 64:128] = part[h:rows]


def unpack(dst, src, rows, columns):
    for start in range(0, columns, 128):
        top = start // 128 * rows
        if start + 128 <= columns:
            dst[:, start:start + 128] = src[top:top + rows, :]
        else:
            h = tail_rows(rows)
            dst[0:h, start:columns] = src[top:top + h, 0:64]
            dst[h:rows, start:columns] = src[top:top + rows - h, 64:128]


def optimizer_kernel(
    Z, Y,
    g_ref, m_ref, v_ref, l_ref, r_ref,
    nm_ref, nv_ref, up_ref,
    g_own, g_all, l_all, r_all, r_pk, part, from_a, from_b, t_own, t_pk, t_all,
    g_in, m_in, v_in, l_in, x_out, f_out, f_in, d_own, d_pk, d_all, b_out, b_in, sib_out, sib_in, u_out, u_in,
    in_sem, out_sem, g_sem, ls_sem, lr_sem, lfs_sem, lfr_sem, rs_sem, rr_sem,
    tas_sem, tar_sem, tbs_sem, tbr_sem, ts_sem, tr_sem, tfs_sem, tfr_sem,
    x_sem, d_sem_s, d_sem_r, b_sem, ss_sem, sr_sem, us_sem, ur_sem, mv_sem,
):
    C = 2
    K = Y * C
    A, B = Z // 2, Z - 1 - Z // 2
    mr = g_ref.shape[0]
    rr, nc = r_ref.shape
    pt = packed_rows(mr, nc)
    row, col = lax.axis_index("row"), lax.axis_index("col")
    xh, z = row // Z, lax.rem(row, Z)
    core = lax.rem(col, C)
    y = lax.rem(col // C, Y)
    xl = col // (C * Y)
    sg = 1 - 2 * core
    rows_me = pl.ds(pl.multiple_of(xh * mr, mr), mr)
    mine = xh == xl

    def wrap(value):
        return lax.rem(value + 4 * Z, Z)

    def device(dxh, dz, dxl, dy, dcore):
        return {"row": dxh * Z + dz, "col": (dxl * Y + dy) * C + dcore}

    ahead = device(xh, wrap(z + sg), xl, y, core)
    behind = device(xh, wrap(z - sg), xl, y, core)
    partner = device(1 - xh, z, xl, y, core)
    sibling = device(xh, z, xl, y, 1 - core)

    def copy(src, dst, send, recv, target):
        return pltpu.make_async_remote_copy(
            src_ref=src, dst_ref=dst, send_sem=send, recv_sem=recv,
            device_id=target, device_id_type=pl.DeviceIdType.MESH,
        )

    barrier = pltpu.get_barrier_semaphore()

    def greet(target):
        pl.semaphore_signal(barrier, inc=1, device_id=target, device_id_type=pl.DeviceIdType.MESH)

    loads = [
        pltpu.make_async_copy(src, dst, in_sem.at[i])
        for i, (src, dst) in enumerate(
            ((g_ref, g_in), (l_ref, l_in), (r_ref, r_all.at[z]), (m_ref, m_in.at[rows_me, :]), (v_ref, v_in.at[rows_me, :]))
        )
    ]
    for load in loads:
        load.start()
    greet(ahead)
    greet(behind)
    for other in range(1, 4 * K):
        place = lax.rem(xh * 2 * K + col + other, 4 * K)
        greet({"row": (place // (2 * K)) * Z + z, "col": lax.rem(place, 2 * K)})

    loads[0].wait()
    g_own[...] = g_in[...].astype(BF16)
    g_all[rows_me, :] = g_own[...]
    slot_me = y * C + core

    loads[1].wait()

    @pl.when(mine)
    def _():
        l_all[slot_me, rows_me, :] = l_in[...]

    pl.semaphore_wait(barrier, 4 * K + 1)

    def to_chips(t):
        dxl, dy = t // Y, t % Y
        here = jnp.logical_and(mine, jnp.logical_and(dxl == xl, dy == y))
        return device(xl, z, dxl, dy, core), jnp.logical_not(here)

    def from_chips(t):
        sxh, sy = t // Y, t % Y
        here = jnp.logical_and(mine, jnp.logical_and(sxh == xh, sy == y))
        return sxh, sy, jnp.logical_not(here)

    def half(dst, side):
        rows = dst.shape[1] // 2
        return pl.ds(pl.multiple_of(side * rows, 16), rows)

    def spread(src, dst, send, recv):
        for t in range(2 * Y):
            target, remote = to_chips(t)

            @pl.when(remote)
            def _():
                copy(src, dst.at[slot_me, half(dst, xh), :], send.at[t], recv.at[xh * Y + y], target).start()

    def spread_wait(src, dst, send, recv):
        for t in range(2 * Y):
            target, remote = to_chips(t)

            @pl.when(remote)
            def _():
                copy(src, dst.at[slot_me, half(dst, xh), :], send.at[t], recv.at[0], target).wait_send()

    def share_copy(dst, t, send, recv, c):
        sxh, sy = t // Y, t % Y
        place = dst.at[sy * C + c, half(dst, sxh), :]
        return copy(place, place, send.at[t], recv.at[t], sibling)

    def share(src, dst, send, recv, fsend, frecv):
        for t in range(2 * Y):
            sxh, sy, remote = from_chips(t)
            place = dst.at[sy * C + core, half(dst, sxh), :]

            @pl.when(remote)
            def _():
                copy(place, place, send.at[0], recv.at[t], sibling).wait_recv()

            share_copy(dst, t, fsend, frecv, core).start()

    def share_wait(dst, fsend, frecv):
        for t in range(2 * Y):
            share_copy(dst, t, fsend, frecv, 1 - core).wait_recv()

    def share_sent(dst, fsend, frecv):
        for t in range(2 * Y):
            share_copy(dst, t, fsend, frecv, core).wait_send()

    r_split = (packed_rows(rr, nc) // 2 + 15) // 16 * 16
    r_cuts = ((0, r_split), (r_split, packed_rows(rr, nc) - r_split))
    chunks = 2

    def r_piece(owner, chunk):
        return r_pk.at[owner, pl.ds(*r_cuts[chunk]), :]

    def r_copy(side, s, chunk):
        if side == 0:
            piece, target = r_piece(wrap(z - sg * (s - 1)), chunk), ahead
        else:
            piece, target = r_piece(wrap(z + sg * (s - 1)), chunk), behind
        index = ((side * A) + s - 1) * chunks + chunk
        return copy(piece, piece, rs_sem.at[index], rr_sem.at[index], target)

    def r_arrival(side, s, chunk):
        piece = r_piece(wrap(z - sg * s) if side == 0 else wrap(z + sg * s), chunk)
        index = ((side * A) + s - 1) * chunks + chunk
        copy(piece, piece, rs_sem.at[index], rr_sem.at[index], ahead).wait_recv()

    started, arrived = set(), set()

    def r_step(n):
        s, chunk = n // chunks + 1, n % chunks
        for side, last in ((0, A), (1, B)):
            if s <= last:
                r_arrival(side, s, chunk)
                arrived.add((side, s, chunk))
                if s < last:
                    r_copy(side, s + 1, chunk).start()
                    started.add((side, s + 1, chunk))
                if chunk == chunks - 1:
                    owner = wrap(z - sg * s) if side == 0 else wrap(z + sg * s)
                    unpack(r_all.at[owner], r_pk.at[owner], rr, nc)


    def finish(level):
        g_copy.wait_send()
        spread_wait(l_in, l_all, ls_sem, lr_sem)
        share_sent(l_all, lfs_sem, lfr_sem)
        for key in sorted(started - arrived):
            r_arrival(*key)
        for key in sorted(started):
            r_copy(*key).wait_send()
        for side, last in ((0, A), (1, B)):
            for s in range(1, last + 1):
                if level >= 4:
                    for i in range(T_N):
                        t_copy(side, s, i)[1].wait_send()
                if level >= 8:
                    for i in range(2):
                        d_copy(side, s, i).wait_send()
        if level >= 5:
            spread_wait(t_own, t_pk, ts_sem, tr_sem)
            share_sent(t_pk, tfs_sem, tfr_sem)
        if 3 <= level < 6:
            for made in moment_copies:
                made.wait()
        if level < 3:
            loads[3].wait()
            loads[4].wait()
        if level >= 6:
            for i in range(2):
                x_copy(i).wait_send()
        if level >= 9:
            b_copy.wait_send()
        if level >= 7:
            for i in range(2):
                for j in range(Y):
                    sib_copy(j, i).wait_send()
                for t in range(2 * Y):
                    made, here = u_copy(t, i)

                    @pl.when(jnp.logical_not(here))
                    def _():
                        made.wait_send()

    g_copy = copy(g_own, g_all.at[rows_me, :], g_sem.at[0], g_sem.at[1], partner)
    if not R_FIRST:
        g_copy.start()
        spread(l_in, l_all, ls_sem, lr_sem)
    loads[2].wait()
    pack(r_pk.at[z], r_all[z], nc)
    for chunk in range(chunks):
        for side, last in ((0, A), (1, B)):
            if last:
                r_copy(side, 1, chunk).start()
                started.add((side, 1, chunk))
    if R_FIRST:
        g_copy.start()
        spread(l_in, l_all, ls_sem, lr_sem)
    steps = A * chunks
    done = 0

    def r_steps(count):
        nonlocal done
        for _ in range(count):
            if done < steps:
                r_step(done)
                done += 1

    share(l_in, l_all, ls_sem, lr_sem, lfs_sem, lfr_sem)
    r_steps(R_START)
    g_copy.wait_recv()
    share_wait(l_all, lfs_sem, lfr_sem)

    loads[3].wait()
    loads[4].wait()
    moment_copies = [
        copy(m_in.at[rows_me, :], m_in.at[rows_me, :], mv_sem.at[0], mv_sem.at[1], partner),
        copy(v_in.at[rows_me, :], v_in.at[rows_me, :], mv_sem.at[2], mv_sem.at[3], partner),
    ]
    for made in moment_copies:
        made.start()

    per = Z // K

    def part_body(i, _):
        k = lax.rem(z // per + K // 2 + i, K)
        value = lax.dot_general(
            l_all[k], g_all[...], (((0,), (0,)), ((), ())), preferred_element_type=F32
        ).astype(BF16)
        for j in range(per):
            pack(part.at[k * per + j], value[j * mr:(j + 1) * mr, :], nc)
        return 0

    lax.fori_loop(0, K, part_body, 0)

    marks = [min(pt, (pt * n // T_N + 15) // 16 * 16) for n in range(T_N + 1)]
    t_cuts = tuple(slice(a, b) for a, b in zip(marks, marks[1:]))

    def t_copy(side, s, i):
        rows, n = t_cuts[i], (s - 1) * T_N + i
        if side == 0:
            d = wrap(z + sg * (A + 1 - s))
            return d, copy(part.at[d, rows, :], from_a.at[s - 1, rows, :], tas_sem.at[n], tar_sem.at[n], ahead)
        d = wrap(z - sg * (B + 1 - s))
        return d, copy(part.at[d, rows, :], from_b.at[s - 1, rows, :], tbs_sem.at[n], tbr_sem.at[n], behind)

    for s in range(1, A + 1):
        for i, rows in enumerate(t_cuts):
            for side, last, came in ((0, A, from_a), (1, B, from_b)):
                if s <= last:
                    d, send = t_copy(side, s, i)
                    if s > 1:
                        t_copy(side, s - 1, i)[1].wait_recv()
                        part[d, rows, :] = (
                            part[d, rows, :].astype(F32) + came[s - 2, rows, :].astype(F32)
                        ).astype(BF16)
                    send.start()
            if i == T_N - 1:
                r_steps(R_FILL[(s - 1) % len(R_FILL)])
    for i, rows in enumerate(t_cuts):
        total = part[z, rows, :].astype(F32)
        if B:
            t_copy(1, B, i)[1].wait_recv()
            total = total + from_b[B - 1, rows, :].astype(F32)
        t_copy(0, A, i)[1].wait_recv()
        total = total + from_a[A - 1, rows, :].astype(F32)
        t_own[rows, :] = total.astype(BF16)

    @pl.when(mine)
    def _():
        t_pk[slot_me, half(t_pk, xh), :] = t_own[...]

    spread(t_own, t_pk, ts_sem, tr_sem)
    r_steps((steps - done) // R_MID if R_MID else 0)
    share(t_own, t_pk, ts_sem, tr_sem, tfs_sem, tfr_sem)
    share_wait(t_pk, tfs_sem, tfr_sem)
    for k in range(K):
        for side in range(2):
            unpack(t_all.at[k, side * mr:(side + 1) * mr, :], t_pk.at[k, side * pt:(side + 1) * pt, :], mr, nc)
    r_steps(steps)

    split = (nc // 2 + 127) // 128 * 128
    cuts = (slice(0, split), slice(split, nc))

    def x_copy(i):
        return copy(b_out.at[:, cuts[i]], b_in.at[:, cuts[i]], x_sem.at[2 * i], x_sem.at[2 * i + 1], partner)

    for i, cut in enumerate(cuts):
        acc = jnp.zeros((2 * mr, cut.stop - cut.start), F32)
        for k in range(K):
            right = r_all[pl.ds(k * per, per), :, cut].reshape(per * r_ref.shape[0], cut.stop - cut.start)
            acc = acc + jnp.dot(t_all[k], right, preferred_element_type=F32)
        x_out[:, cut] = acc
        b_out[:, cut] = acc.astype(BF16)
        x_copy(i).start()

    first_fix = 1.0 - beta_first**STEP
    second_fix = 1.0 - beta_second**STEP
    for made in moment_copies:
        made.wait()
    for i, cut in enumerate(cuts):
        x_copy(i).wait_recv()
        rotated = x_out[:, cut] + b_in[:, cut].astype(F32)
        new_moment = beta_first * m_in[:, cut] + (1.0 - beta_first) * rotated
        new_second = beta_second * v_in[:, cut] + (1.0 - beta_second) * rotated * rotated
        direction = new_moment / first_fix / (jnp.sqrt(new_second / second_fix) + epsilon_add)
        d_own[:, cut] = direction.astype(BF16)
        m_in[:, cut] = new_moment
        v_in[:, cut] = new_second

    packs = (slice(0, split // 128 * mr), slice(split // 128 * mr, pt))

    def update_block(k, cut):
        right = r_all[pl.ds(k * per, per)].reshape(per * rr, nc)[cut]
        return lax.dot_general(d_own[...], right, (((1,), (1,)), ((), ())), preferred_element_type=F32)

    def sib_copy(j, i):
        n = j * 2 + i
        return copy(sib_out.at[j, :, cuts[i]], sib_in.at[j, :, cuts[i]], ss_sem.at[n], sr_sem.at[n], sibling)

    for i, cut in enumerate(cuts):
        for j in range(Y):
            sib_out[j, :, cut] = update_block(j * C + 1 - core, cut).astype(BF16)
            sib_copy(j, i).start()

    def u_copy(t, i):
        txh, ty = t // Y, t % Y
        here = jnp.logical_and(mine, jnp.logical_and(txh == xh, ty == y))
        made = copy(
            u_out.at[ty, txh, packs[i], :], u_in.at[xl * Y + y, packs[i], :],
            us_sem.at[t * 2 + i], ur_sem.at[(xl * Y + y) * 2 + i], device(txh, z, xh, ty, core),
        )
        return made, here

    for i, cut in enumerate(cuts):
        for j in range(Y):
            value = update_block(j * C + core, cut)
            sib_copy(j, i).wait_recv()
            value = (value + sib_in[j, :, cut].astype(F32)).astype(BF16)
            for txh in range(2):
                pack(u_out.at[j, txh], value[txh * mr:(txh + 1) * mr], nc, cut.start)
            for txh in range(2):
                made, here = u_copy(txh * Y + j, i)

                @pl.when(jnp.logical_not(here))
                def _():
                    made.start()

        @pl.when(mine)
        def _():
            u_in[xl * Y + y, packs[i], :] = u_out[y, xh, packs[i], :]

    nm_ref[...] = m_in[rows_me, :]
    nv_ref[...] = v_in[rows_me, :]

    def d_piece(owner, i):
        return d_pk.at[owner, packs[i], :]

    def d_copy(side, s, i):
        owner, target = (wrap(z - sg * (s - 1)), ahead) if side == 0 else (wrap(z + sg * (s - 1)), behind)
        index = (side * A + s - 1) * 2 + i
        piece = d_piece(owner, i)
        return copy(piece, piece, d_sem_s.at[index], d_sem_r.at[index], target)

    def d_step(s, i):
        for side, last in ((0, A), (1, B)):
            if 1 <= s <= last:
                piece = d_piece(wrap(z - sg * s) if side == 0 else wrap(z + sg * s), i)
                index = (side * A + s - 1) * 2 + i
                copy(piece, piece, d_sem_s.at[index], d_sem_r.at[index], ahead).wait_recv()
            if s < last:
                d_copy(side, s + 1, i).start()
            if i == 1 and 1 <= s <= last:
                owner = wrap(z - sg * s) if side == 0 else wrap(z + sg * s)
                unpack(d_all.at[owner], d_pk.at[owner], mr, nc)

    def own_sum(i):
        rows = packs[i]
        total = jnp.zeros((rows.stop - rows.start, 128), F32)
        for t in range(2 * Y):
            here = jnp.logical_and(mine, jnp.logical_and(t // Y == xl, t % Y == y))

            @pl.when(jnp.logical_not(here))
            def _():
                copy(
                    u_in.at[t, rows, :], u_in.at[t, rows, :], us_sem.at[0], ur_sem.at[t * 2 + i], sibling
                ).wait_recv()

            total = total + u_in[t, rows, :].astype(F32)
        d_pk[z, rows, :] = total.astype(BF16)
        if i == 1:
            unpack(d_all.at[z], d_pk.at[z], mr, nc)

    own_sum(0)
    d_step(0, 0)
    for s in range(1, E_EARLY + 1):
        d_step(s, 0)
    own_sum(1)
    d_step(0, 1)
    for s in range(1, A + 1):
        if s + E_EARLY <= A:
            d_step(s + E_EARLY, 0)
        d_step(s, 1)
    rows_other = pl.ds(pl.multiple_of((1 - xh) * mr, mr), mr)

    def left_product(rows):
        acc = jnp.zeros((mr, nc), F32)
        for k in range(K):
            acc = acc + jnp.dot(
                l_all[k, rows, :], d_all[pl.ds(k * per, per)].reshape(per * mr, nc), preferred_element_type=F32
            )
        return acc

    f_out[...] = left_product(rows_other).astype(BF16)
    b_copy = copy(f_out, f_in, b_sem.at[0], b_sem.at[1], partner)
    b_copy.start()
    own = left_product(rows_me)
    b_copy.wait_recv()
    up_ref[...] = own + f_in[...].astype(F32)
    finish(9)


def per_device(Z, Y, gradient, moment, second, left_basis, right_basis):
    mr, nc = gradient.shape
    K = 2 * Y
    A, B = Z // 2, Z - 1 - Z // 2
    rr = right_basis.shape[0]
    lc = left_basis.shape[1]
    per = Z // K
    chunks = 2
    pt = packed_rows(mr, nc)
    V = pltpu.VMEM
    DMA = pltpu.SemaphoreType.DMA
    vmem = pl.BlockSpec(memory_space=pltpu.VMEM)
    out = jax.ShapeDtypeStruct((mr, nc), F32)
    return pl.pallas_call(
        functools.partial(optimizer_kernel, Z, Y),
        out_shape=(out, out, out),
        in_specs=[pl.BlockSpec(memory_space=pltpu.HBM)] * 5,
        out_specs=(vmem, vmem, vmem),
        scratch_shapes=[
            V((mr, nc), BF16),
            V((2 * mr, nc), BF16),
            V((K, 2 * mr, lc), BF16),
            V((Z, rr, nc), BF16),
            V((Z, packed_rows(rr, nc), 128), BF16),
            V((Z, pt, 128), BF16),
            V((A, pt, 128), BF16),
            V((max(B, 1), pt, 128), BF16),
            V((pt, 128), BF16),
            V((K, 2 * pt, 128), BF16),
            V((K, 2 * mr, nc), BF16),
            V((mr, nc), F32),
            V((2 * mr, nc), F32),
            V((2 * mr, nc), F32),
            V((mr, lc), BF16),
            V((2 * mr, nc), F32),
            V((mr, nc), BF16),
            V((mr, nc), BF16),
            V((2 * mr, nc), BF16),
            V((Z, pt, 128), BF16),
            V((Z, mr, nc), BF16),
            V((2 * mr, nc), BF16),
            V((2 * mr, nc), BF16),
            V((Y, 2 * mr, nc), BF16),
            V((Y, 2 * mr, nc), BF16),
            V((Y, 2, pt, 128), BF16),
            V((2 * Y, pt, 128), BF16),
            DMA((5,)),
            DMA((3,)),
            DMA((2,)),
            DMA((2 * Y,)), DMA((2 * Y,)), DMA((2 * Y,)), DMA((2 * Y,)),
            DMA(((A + B) * chunks,)), DMA(((A + B) * chunks,)),
            DMA((T_N * A,)), DMA((T_N * A,)), DMA((T_N * max(B, 1),)), DMA((T_N * max(B, 1),)),
            DMA((2 * Y,)), DMA((2 * Y,)), DMA((2 * Y,)), DMA((2 * Y,)),
            DMA((4,)),
            DMA((2 * A + 2 * B,)), DMA((2 * A + 2 * B,)),
            DMA((2,)),
            DMA((2 * Y,)), DMA((2 * Y,)),
            DMA((4 * Y,)), DMA((4 * Y,)),
            DMA((4,)),
        ],
        compiler_params=pltpu.CompilerParams(
            collective_id=0, has_side_effects=True, vmem_limit_bytes=int(63.5 * 1024 * 1024)
        ),
    )(gradient, moment, second, left_basis, right_basis)


def solution(mesh):
    Z, Y = mesh.shape["row"] // 2, mesh.shape["col"] // 4
    return jax.shard_map(
        functools.partial(per_device, Z, Y),
        mesh=mesh,
        in_specs=(
            P("row", "col"),
            P("row", "col"),
            P("row", "col"),
            P("row", "col"),
            P("row", "col"),
        ),
        out_specs=(P("row", "col"), P("row", "col"), P("row", "col")),
        check_vma=False,
    )
```

```python
import functools

import jax
import jax.numpy as jnp
from jax import lax
from jax.experimental import pallas as pl
from jax.experimental.pallas import tpu as pltpu
from jax.sharding import PartitionSpec as P

STEP = 100
R_START = 2
T_N = 1
E_EARLY = 0
R_FIRST = True
R_FILL = (1,)


beta_first = 0.9
beta_second = 0.99
epsilon_add = 1e-08

F32 = jnp.float32
BF16 = jnp.bfloat16


def tail_rows(rows):
    return (rows // 2 + 15) // 16 * 16


def packed_rows(rows, columns):
    return columns // 128 * rows + (tail_rows(rows) if columns % 128 else 0)


def pack(dst, value, columns, first=0):
    rows = value.shape[0]
    for start in range(first, first + value.shape[1], 128):
        top, part = start // 128 * rows, value[:, start - first:min(start + 128, columns) - first]
        if start + 128 <= columns:
            dst[top:top + rows, :] = part
        else:
            h = tail_rows(rows)
            dst[top:top + h, 0:64] = part[0:h]
            dst[top:top + rows - h, 64:128] = part[h:rows]


def unpack(dst, src, rows, columns):
    for start in range(0, columns, 128):
        top = start // 128 * rows
        if start + 128 <= columns:
            dst[:, start:start + 128] = src[top:top + rows, :]
        else:
            h = tail_rows(rows)
            dst[0:h, start:columns] = src[top:top + h, 0:64]
            dst[h:rows, start:columns] = src[top:top + rows - h, 64:128]


def optimizer_kernel(
    Z, Y,
    g_ref, m_ref, v_ref, l_ref, r_ref,
    nm_ref, nv_ref, up_ref,
    g_own, g_all, l_all, r_all, r_pk, part, from_a, from_b, t_own, t_pk, t_all,
    g_in, m_in, v_in, l_in, x_out, f_out, f_in, d_own, d_pk, d_all, b_out, b_in, sib_out, sib_in, u_out, u_in,
    in_sem, out_sem, g_sem, ls_sem, lr_sem, lfs_sem, lfr_sem, rs_sem, rr_sem,
    tas_sem, tar_sem, tbs_sem, tbr_sem, ts_sem, tr_sem, tfs_sem, tfr_sem,
    x_sem, d_sem_s, d_sem_r, b_sem, ss_sem, sr_sem, us_sem, ur_sem, mv_sem,
):
    C = 2
    K = Y * C
    A, B = Z // 2, Z - 1 - Z // 2
    mr = g_ref.shape[0]
    rr, nc = r_ref.shape
    pt = packed_rows(mr, nc)
    row, col = lax.axis_index("row"), lax.axis_index("col")
    xh, z = row // Z, lax.rem(row, Z)
    core = lax.rem(col, C)
    y = lax.rem(col // C, Y)
    xl = col // (C * Y)
    sg = 1 - 2 * core
    rows_me = pl.ds(pl.multiple_of(xh * mr, mr), mr)
    mine = xh == xl

    def wrap(value):
        return lax.rem(value + 4 * Z, Z)

    def device(dxh, dz, dxl, dy, dcore):
        return {"row": dxh * Z + dz, "col": (dxl * Y + dy) * C + dcore}

    ahead = device(xh, wrap(z + sg), xl, y, core)
    behind = device(xh, wrap(z - sg), xl, y, core)
    partner = device(1 - xh, z, xl, y, core)
    sibling = device(xh, z, xl, y, 1 - core)

    def copy(src, dst, send, recv, target):
        return pltpu.make_async_remote_copy(
            src_ref=src, dst_ref=dst, send_sem=send, recv_sem=recv,
            device_id=target, device_id_type=pl.DeviceIdType.MESH,
        )

    barrier = pltpu.get_barrier_semaphore()

    def greet(target):
        pl.semaphore_signal(barrier, inc=1, device_id=target, device_id_type=pl.DeviceIdType.MESH)

    loads = [
        pltpu.make_async_copy(src, dst, in_sem.at[i])
        for i, (src, dst) in enumerate(
            ((g_ref, g_in), (l_ref, l_in), (r_ref, r_all.at[z]), (m_ref, m_in.at[rows_me, :]), (v_ref, v_in.at[rows_me, :]))
        )
    ]
    for load in loads:
        load.start()
    greet(ahead)
    greet(behind)
    for other in range(1, 4 * K):
        place = lax.rem(xh * 2 * K + col + other, 4 * K)
        greet({"row": (place // (2 * K)) * Z + z, "col": lax.rem(place, 2 * K)})

    loads[0].wait()
    g_own[...] = g_in[...].astype(BF16)
    g_all[rows_me, :] = g_own[...]
    slot_me = y * C + core

    loads[1].wait()

    @pl.when(mine)
    def _():
        l_all[slot_me, rows_me, :] = l_in[...]

    pl.semaphore_wait(barrier, 4 * K + 1)

    def to_chips(t):
        dxl, dy = t // Y, t % Y
        here = jnp.logical_and(mine, jnp.logical_and(dxl == xl, dy == y))
        return device(xl, z, dxl, dy, core), jnp.logical_not(here)

    def from_chips(t):
        sxh, sy = t // Y, t % Y
        here = jnp.logical_and(mine, jnp.logical_and(sxh == xh, sy == y))
        return sxh, sy, jnp.logical_not(here)

    def half(dst, side):
        rows = dst.shape[1] // 2
        return pl.ds(pl.multiple_of(side * rows, 16), rows)

    def spread(src, dst, send, recv):
        for t in range(2 * Y):
            target, remote = to_chips(t)

            @pl.when(remote)
            def _():
                copy(src, dst.at[slot_me, half(dst, xh), :], send.at[t], recv.at[xh * Y + y], target).start()

    def spread_wait(src, dst, send, recv):
        for t in range(2 * Y):
            target, remote = to_chips(t)

            @pl.when(remote)
            def _():
                copy(src, dst.at[slot_me, half(dst, xh), :], send.at[t], recv.at[0], target).wait_send()

    def share_copy(dst, t, send, recv, c):
        sxh, sy = t // Y, t % Y
        place = dst.at[sy * C + c, half(dst, sxh), :]
        return copy(place, place, send.at[t], recv.at[t], sibling)

    def share(src, dst, send, recv, fsend, frecv):
        for t in range(2 * Y):
            sxh, sy, remote = from_chips(t)
            place = dst.at[sy * C + core, half(dst, sxh), :]

            @pl.when(remote)
            def _():
                copy(place, place, send.at[0], recv.at[t], sibling).wait_recv()

            share_copy(dst, t, fsend, frecv, core).start()

    def share_wait(dst, fsend, frecv):
        for t in range(2 * Y):
            share_copy(dst, t, fsend, frecv, 1 - core).wait_recv()

    def share_sent(dst, fsend, frecv):
        for t in range(2 * Y):
            share_copy(dst, t, fsend, frecv, core).wait_send()

    r_split = (packed_rows(rr, nc) // 2 + 15) // 16 * 16
    r_cuts = ((0, r_split), (r_split, packed_rows(rr, nc) - r_split))
    chunks = 2

    def r_piece(owner, chunk):
        return r_pk.at[owner, pl.ds(*r_cuts[chunk]), :]

    def r_copy(side, s, chunk):
        if side == 0:
            piece, target = r_piece(wrap(z - sg * (s - 1)), chunk), ahead
        else:
            piece, target = r_piece(wrap(z + sg * (s - 1)), chunk), behind
        index = ((side * A) + s - 1) * chunks + chunk
        return copy(piece, piece, rs_sem.at[index], rr_sem.at[index], target)

    def r_arrival(side, s, chunk):
        piece = r_piece(wrap(z - sg * s) if side == 0 else wrap(z + sg * s), chunk)
        index = ((side * A) + s - 1) * chunks + chunk
        copy(piece, piece, rs_sem.at[index], rr_sem.at[index], ahead).wait_recv()

    started, arrived = set(), set()

    def r_step(n):
        s, chunk = n // chunks + 1, n % chunks
        for side, last in ((0, A), (1, B)):
            if s <= last:
                r_arrival(side, s, chunk)
                arrived.add((side, s, chunk))
                if s < last:
                    r_copy(side, s + 1, chunk).start()
                    started.add((side, s + 1, chunk))
                if chunk == chunks - 1:
                    owner = wrap(z - sg * s) if side == 0 else wrap(z + sg * s)
                    unpack(r_all.at[owner], r_pk.at[owner], rr, nc)


    def finish(level):
        g_copy.wait_send()
        spread_wait(l_in, l_all, ls_sem, lr_sem)
        share_sent(l_all, lfs_sem, lfr_sem)
        for key in sorted(started - arrived):
            r_arrival(*key)
        for key in sorted(started):
            r_copy(*key).wait_send()
        for side, last in ((0, A), (1, B)):
            for s in range(1, last + 1):
                if level >= 4:
                    for i in range(T_N):
                        t_copy(side, s, i)[1].wait_send()
                if level >= 8:
                    for i in range(2):
                        d_copy(side, s, i).wait_send()
        if level >= 5:
            spread_wait(t_own, t_pk, ts_sem, tr_sem)
            share_sent(t_pk, tfs_sem, tfr_sem)
        if 3 <= level < 6:
            for made in moment_copies:
                made.wait()
        if level < 3:
            loads[3].wait()
            loads[4].wait()
        if level >= 6:
            for i in range(2):
                x_copy(i).wait_send()
        if level >= 9:
            b_copy.wait_send()
        if level >= 7:
            for i in range(2):
                for j in range(Y):
                    sib_copy(j, i).wait_send()
                for t in range(2 * Y):
                    made, here = u_copy(t, i)

                    @pl.when(jnp.logical_not(here))
                    def _():
                        made.wait_send()

    g_copy = copy(g_own, g_all.at[rows_me, :], g_sem.at[0], g_sem.at[1], partner)
    if not R_FIRST:
        g_copy.start()
        spread(l_in, l_all, ls_sem, lr_sem)
    loads[2].wait()
    pack(r_pk.at[z], r_all[z], nc)
    for chunk in range(chunks):
        for side, last in ((0, A), (1, B)):
            if last:
                r_copy(side, 1, chunk).start()
                started.add((side, 1, chunk))
    if R_FIRST:
        g_copy.start()
        spread(l_in, l_all, ls_sem, lr_sem)
    steps = A * chunks
    done = 0

    def r_steps(count):
        nonlocal done
        for _ in range(count):
            if done < steps:
                r_step(done)
                done += 1

    share(l_in, l_all, ls_sem, lr_sem, lfs_sem, lfr_sem)
    r_steps(R_START)
    g_copy.wait_recv()
    share_wait(l_all, lfs_sem, lfr_sem)

    loads[3].wait()
    loads[4].wait()
    moment_copies = [
        copy(m_in.at[rows_me, :], m_in.at[rows_me, :], mv_sem.at[0], mv_sem.at[1], partner),
        copy(v_in.at[rows_me, :], v_in.at[rows_me, :], mv_sem.at[2], mv_sem.at[3], partner),
    ]
    for made in moment_copies:
        made.start()

    per = Z // K

    def part_body(i, _):
        k = lax.rem(z // per + K // 2 + i, K)
        value = lax.dot_general(
            l_all[k], g_all[...], (((0,), (0,)), ((), ())), preferred_element_type=F32
        ).astype(BF16)
        for j in range(per):
            pack(part.at[k * per + j], value[j * mr:(j + 1) * mr, :], nc)
        return 0

    lax.fori_loop(0, K, part_body, 0)

    marks = [min(pt, (pt * n // T_N + 15) // 16 * 16) for n in range(T_N + 1)]
    t_cuts = tuple(slice(a, b) for a, b in zip(marks, marks[1:]))

    def t_copy(side, s, i):
        rows, n = t_cuts[i], (s - 1) * T_N + i
        if side == 0:
            d = wrap(z + sg * (A + 1 - s))
            return d, copy(part.at[d, rows, :], from_a.at[s - 1, rows, :], tas_sem.at[n], tar_sem.at[n], ahead)
        d = wrap(z - sg * (B + 1 - s))
        return d, copy(part.at[d, rows, :], from_b.at[s - 1, rows, :], tbs_sem.at[n], tbr_sem.at[n], behind)

    for s in range(1, A + 1):
        for i, rows in enumerate(t_cuts):
            for side, last, came in ((0, A, from_a), (1, B, from_b)):
                if s <= last:
                    d, send = t_copy(side, s, i)
                    if s > 1:
                        t_copy(side, s - 1, i)[1].wait_recv()
                        part[d, rows, :] = (
                            part[d, rows, :].astype(F32) + came[s - 2, rows, :].astype(F32)
                        ).astype(BF16)
                    send.start()
            if i == T_N - 1:
                r_steps(R_FILL[(s - 1) % len(R_FILL)])
    for i, rows in enumerate(t_cuts):
        total = part[z, rows, :].astype(F32)
        if B:
            t_copy(1, B, i)[1].wait_recv()
            total = total + from_b[B - 1, rows, :].astype(F32)
        t_copy(0, A, i)[1].wait_recv()
        total = total + from_a[A - 1, rows, :].astype(F32)
        t_own[rows, :] = total.astype(BF16)

    @pl.when(mine)
    def _():
        t_pk[slot_me, half(t_pk, xh), :] = t_own[...]

    spread(t_own, t_pk, ts_sem, tr_sem)
    r_steps(max(steps - done - chunks, 0))
    share(t_own, t_pk, ts_sem, tr_sem, tfs_sem, tfr_sem)
    share_wait(t_pk, tfs_sem, tfr_sem)
    for k in range(K):
        for side in range(2):
            unpack(t_all.at[k, side * mr:(side + 1) * mr, :], t_pk.at[k, side * pt:(side + 1) * pt, :], mr, nc)
    r_steps(steps)

    split = (nc // 2 + 127) // 128 * 128
    cuts = (slice(0, split), slice(split, nc))

    def x_copy(i):
        return copy(b_out.at[:, cuts[i]], b_in.at[:, cuts[i]], x_sem.at[2 * i], x_sem.at[2 * i + 1], partner)

    for i, cut in enumerate(cuts):
        acc = jnp.zeros((2 * mr, cut.stop - cut.start), F32)
        for k in range(K):
            right = r_all[pl.ds(k * per, per), :, cut].reshape(per * r_ref.shape[0], cut.stop - cut.start)
            acc = acc + jnp.dot(t_all[k], right, preferred_element_type=F32)
        x_out[:, cut] = acc
        b_out[:, cut] = acc.astype(BF16)
        x_copy(i).start()

    first_fix = 1.0 - beta_first**STEP
    second_fix = 1.0 - beta_second**STEP
    for made in moment_copies:
        made.wait()
    for i, cut in enumerate(cuts):
        x_copy(i).wait_recv()
        rotated = x_out[:, cut] + b_in[:, cut].astype(F32)
        new_moment = beta_first * m_in[:, cut] + (1.0 - beta_first) * rotated
        new_second = beta_second * v_in[:, cut] + (1.0 - beta_second) * rotated * rotated
        direction = new_moment / first_fix / (jnp.sqrt(new_second / second_fix) + epsilon_add)
        d_own[:, cut] = direction.astype(BF16)
        m_in[:, cut] = new_moment
        v_in[:, cut] = new_second

    packs = (slice(0, split // 128 * mr), slice(split // 128 * mr, pt))

    def update_block(k, cut):
        right = r_all[pl.ds(k * per, per)].reshape(per * rr, nc)[cut]
        return lax.dot_general(d_own[...], right, (((1,), (1,)), ((), ())), preferred_element_type=F32)

    def sib_copy(j, i):
        n = j * 2 + i
        return copy(sib_out.at[j, :, cuts[i]], sib_in.at[j, :, cuts[i]], ss_sem.at[n], sr_sem.at[n], sibling)

    for i, cut in enumerate(cuts):
        for j in range(Y):
            sib_out[j, :, cut] = update_block(j * C + 1 - core, cut).astype(BF16)
            sib_copy(j, i).start()

    def u_copy(t, i):
        txh, ty = t // Y, t % Y
        here = jnp.logical_and(mine, jnp.logical_and(txh == xh, ty == y))
        made = copy(
            u_out.at[ty, txh, packs[i], :], u_in.at[xl * Y + y, packs[i], :],
            us_sem.at[t * 2 + i], ur_sem.at[(xl * Y + y) * 2 + i], device(txh, z, xh, ty, core),
        )
        return made, here

    for i, cut in enumerate(cuts):
        for j in range(Y):
            value = update_block(j * C + core, cut)
            sib_copy(j, i).wait_recv()
            value = (value + sib_in[j, :, cut].astype(F32)).astype(BF16)
            for txh in range(2):
                pack(u_out.at[j, txh], value[txh * mr:(txh + 1) * mr], nc, cut.start)
            for txh in range(2):
                made, here = u_copy(txh * Y + j, i)

                @pl.when(jnp.logical_not(here))
                def _():
                    made.start()

        @pl.when(mine)
        def _():
            u_in[xl * Y + y, packs[i], :] = u_out[y, xh, packs[i], :]

    nm_ref[...] = m_in[rows_me, :]
    nv_ref[...] = v_in[rows_me, :]

    def d_piece(owner, i):
        return d_pk.at[owner, packs[i], :]

    def d_copy(side, s, i):
        owner, target = (wrap(z - sg * (s - 1)), ahead) if side == 0 else (wrap(z + sg * (s - 1)), behind)
        index = (side * A + s - 1) * 2 + i
        piece = d_piece(owner, i)
        return copy(piece, piece, d_sem_s.at[index], d_sem_r.at[index], target)

    def d_step(s, i):
        for side, last in ((0, A), (1, B)):
            if 1 <= s <= last:
                piece = d_piece(wrap(z - sg * s) if side == 0 else wrap(z + sg * s), i)
                index = (side * A + s - 1) * 2 + i
                copy(piece, piece, d_sem_s.at[index], d_sem_r.at[index], ahead).wait_recv()
            if s < last:
                d_copy(side, s + 1, i).start()
            if i == 1 and 1 <= s <= last:
                owner = wrap(z - sg * s) if side == 0 else wrap(z + sg * s)
                unpack(d_all.at[owner], d_pk.at[owner], mr, nc)

    def own_sum(i):
        rows = packs[i]
        total = jnp.zeros((rows.stop - rows.start, 128), F32)
        for t in range(2 * Y):
            here = jnp.logical_and(mine, jnp.logical_and(t // Y == xl, t % Y == y))

            @pl.when(jnp.logical_not(here))
            def _():
                copy(
                    u_in.at[t, rows, :], u_in.at[t, rows, :], us_sem.at[0], ur_sem.at[t * 2 + i], sibling
                ).wait_recv()

            total = total + u_in[t, rows, :].astype(F32)
        d_pk[z, rows, :] = total.astype(BF16)
        if i == 1:
            unpack(d_all.at[z], d_pk.at[z], mr, nc)

    own_sum(0)
    d_step(0, 0)
    for s in range(1, E_EARLY + 1):
        d_step(s, 0)
    own_sum(1)
    d_step(0, 1)
    for s in range(1, A + 1):
        if s + E_EARLY <= A:
            d_step(s + E_EARLY, 0)
        d_step(s, 1)
    rows_other = pl.ds(pl.multiple_of((1 - xh) * mr, mr), mr)

    def left_product(rows):
        acc = jnp.zeros((mr, nc), F32)
        for k in range(K):
            acc = acc + jnp.dot(
                l_all[k, rows, :], d_all[pl.ds(k * per, per)].reshape(per * mr, nc), preferred_element_type=F32
            )
        return acc

    f_out[...] = left_product(rows_other).astype(BF16)
    b_copy = copy(f_out, f_in, b_sem.at[0], b_sem.at[1], partner)
    b_copy.start()
    own = left_product(rows_me)
    b_copy.wait_recv()
    up_ref[...] = own + f_in[...].astype(F32)
    finish(9)


def per_device(Z, Y, gradient, moment, second, left_basis, right_basis):
    mr, nc = gradient.shape
    K = 2 * Y
    A, B = Z // 2, Z - 1 - Z // 2
    rr = right_basis.shape[0]
    lc = left_basis.shape[1]
    per = Z // K
    chunks = 2
    pt = packed_rows(mr, nc)
    V = pltpu.VMEM
    DMA = pltpu.SemaphoreType.DMA
    vmem = pl.BlockSpec(memory_space=pltpu.VMEM)
    out = jax.ShapeDtypeStruct((mr, nc), F32)
    return pl.pallas_call(
        functools.partial(optimizer_kernel, Z, Y),
        out_shape=(out, out, out),
        in_specs=[pl.BlockSpec(memory_space=pltpu.HBM)] * 5,
        out_specs=(vmem, vmem, vmem),
        scratch_shapes=[
            V((mr, nc), BF16),
            V((2 * mr, nc), BF16),
            V((K, 2 * mr, lc), BF16),
            V((Z, rr, nc), BF16),
            V((Z, packed_rows(rr, nc), 128), BF16),
            V((Z, pt, 128), BF16),
            V((A, pt, 128), BF16),
            V((max(B, 1), pt, 128), BF16),
            V((pt, 128), BF16),
            V((K, 2 * pt, 128), BF16),
            V((K, 2 * mr, nc), BF16),
            V((mr, nc), F32),
            V((2 * mr, nc), F32),
            V((2 * mr, nc), F32),
            V((mr, lc), BF16),
            V((2 * mr, nc), F32),
            V((mr, nc), BF16),
            V((mr, nc), BF16),
            V((2 * mr, nc), BF16),
            V((Z, pt, 128), BF16),
            V((Z, mr, nc), BF16),
            V((2 * mr, nc), BF16),
            V((2 * mr, nc), BF16),
            V((Y, 2 * mr, nc), BF16),
            V((Y, 2 * mr, nc), BF16),
            V((Y, 2, pt, 128), BF16),
            V((2 * Y, pt, 128), BF16),
            DMA((5,)),
            DMA((3,)),
            DMA((2,)),
            DMA((2 * Y,)), DMA((2 * Y,)), DMA((2 * Y,)), DMA((2 * Y,)),
            DMA(((A + B) * chunks,)), DMA(((A + B) * chunks,)),
            DMA((T_N * A,)), DMA((T_N * A,)), DMA((T_N * max(B, 1),)), DMA((T_N * max(B, 1),)),
            DMA((2 * Y,)), DMA((2 * Y,)), DMA((2 * Y,)), DMA((2 * Y,)),
            DMA((4,)),
            DMA((2 * A + 2 * B,)), DMA((2 * A + 2 * B,)),
            DMA((2,)),
            DMA((2 * Y,)), DMA((2 * Y,)),
            DMA((4 * Y,)), DMA((4 * Y,)),
            DMA((4,)),
        ],
        compiler_params=pltpu.CompilerParams(
            collective_id=0, has_side_effects=True, vmem_limit_bytes=int(63.5 * 1024 * 1024)
        ),
    )(gradient, moment, second, left_basis, right_basis)


def solution(mesh):
    Z, Y = mesh.shape["row"] // 2, mesh.shape["col"] // 4
    return jax.shard_map(
        functools.partial(per_device, Z, Y),
        mesh=mesh,
        in_specs=(
            P("row", "col"),
            P("row", "col"),
            P("row", "col"),
            P("row", "col"),
            P("row", "col"),
        ),
        out_specs=(P("row", "col"), P("row", "col"), P("row", "col")),
        check_vma=False,
    )
```
